32 devices in a mesh: groups: 2 (over y), ex: 8 (over z, x), proj: 2 (over core).
Axes of the slice: x: 2, y: 2, z: 4, core: 2. Of those that a mesh axis runs over, the one named last changes fastest.
Arguments:
- train_factors: bfloat16 [16384, 4, 128], P(('groups', 'ex'), 'proj'), parts along dimension 0, may hold values from -600 to 600, as said below
- query_grads: float32 [256, 4, 4096], P(('groups', 'ex'), 'proj'), parts along dimension 0, may hold values from -600 to 600, as said below
Outputs:
- scores: float32 [16384, 128], P(('groups', 'ex'), 'proj'), parts along dimension 0
The draws below stay inside these ranges and needn't reach their ends.
There are 2 independent parts, one for each index of `groups`. The reference program is written for one: setup_inputs(seed, part) draws one part's arguments, and reference() takes and returns one part's arrays. A program takes and returns all parts, laid end to end along the dimension named above; each array names one. Nothing has to cross between parts.
Inputs may be any that keep to these rules, and one draw needn't show every extreme that they name: `train_factors`: real-valued projected factors of mixed scale. `query_grads`: real-valued projected gradients of mixed scale.
All inputs are finite; a program needn't handle non-finite values.
Results may differ from the reference program's by a relative error of at most 0.005.
Values may be sent and summed in bfloat16 or wider, within the bound.
No kernel may reach another device: no remote copies, remote signals or barrier semaphores. Data moves between devices by JAX's collectives and lax.ppermute only.
A program may use at most 64 MiB of HBM per device.

```python
import math
import jax
import jax.numpy as jnp
from jax import lax

RANK = 64
MODULES = 4
NQ = 128
T_DEV = 1024
TOKENS = 8192
K = 16384
N_EX = 8


def scaled_array(key, shape):
    first, second, third = jax.random.split(key, 3)
    base = jax.random.truncated_normal(first, -5.0, 5.0, shape, jnp.float32)
    row_shape = (shape[0],) + (1,) * (len(shape) - 1)
    col_shape = (1,) + tuple(shape[1:])
    row_scale = jnp.exp(jax.random.uniform(second, row_shape, jnp.float32) * math.log(10.0))
    col_scale = jnp.exp(jax.random.uniform(third, col_shape, jnp.float32) * math.log(10.0))
    return base * row_scale * col_scale


def draw_train_factors(key, part):
    key = jax.random.fold_in(key, 11)
    return scaled_array(key, (TOKENS, MODULES, 2 * RANK)).astype(jnp.bfloat16)


def draw_query_grads(key, part):
    key = jax.random.fold_in(key, 23)
    return scaled_array(key, (NQ, MODULES, RANK * RANK))


def setup_inputs(seed: int = 0, part: int = 0) -> dict:
    key_of = jax.random.split(jax.random.key(seed), 3)
    own_keys = jax.random.split(jax.random.fold_in(key_of[2], part), 3)
    return {
        "train_factors": draw_train_factors(jax.random.fold_in(jax.random.fold_in(key_of[2], part), 71), part),
        "query_grads": draw_query_grads(jax.random.fold_in(jax.random.fold_in(key_of[2], part), 71), part),
    }


epsilon = 1e-06

def reference(train_factors, query_grads):
    query_sq = lax.optimization_barrier(jnp.mean(query_grads * query_grads, axis=(1, 2)))
    query_unit = (query_grads * lax.rsqrt(query_sq + epsilon)[:, None, None]).astype(jnp.bfloat16)
    query_mats = query_unit.reshape(NQ, MODULES, RANK, RANK).astype(jnp.float32)
    act_all = train_factors[:, :, :RANK].astype(jnp.float32)
    grad_all = train_factors[:, :, RANK:].astype(jnp.float32)
    token_norm = lax.optimization_barrier(jnp.sum(lax.optimization_barrier(jnp.sum(act_all * act_all, axis=2)) * lax.optimization_barrier(jnp.sum(grad_all * grad_all, axis=2)), axis=1))
    train_scale = lax.rsqrt(token_norm / K + epsilon)
    blocks = train_factors.reshape(N_EX * (T_DEV // 8), 8, MODULES, 2 * RANK)

    def one_block(rows):
        act_rows = rows[:, :, :RANK].astype(jnp.float32)
        grad_rows = rows[:, :, RANK:].astype(jnp.float32)
        inner = jnp.einsum('tmj,qmij->tmqi', grad_rows, query_mats, precision=lax.Precision.HIGHEST)
        inner = inner.astype(jnp.bfloat16).astype(jnp.float32)
        return jnp.einsum('tmi,tmqi->tq', act_rows, inner, precision=lax.Precision.HIGHEST)
    raw = lax.map(one_block, blocks).reshape(TOKENS, NQ)
    return raw * (train_scale / jnp.sqrt(jnp.float32(K)))[:, None]
```

```python
import functools

import jax
import jax.numpy as jnp
from jax import lax
from jax.experimental import pallas as pl
from jax.experimental.pallas import tpu as pltpu
from jax.sharding import PartitionSpec as P

epsilon = 1e-06
LANES = 128
GROUP = 16
VMEM = pl.BlockSpec(memory_space=pltpu.VMEM)
PARAMS = pltpu.CompilerParams(vmem_limit_bytes=32 * 1024 * 1024)


def query_kernel(modules, pairs, x_ref, o_ref):
    queries = o_ref.shape[1]
    for m in range(modules):
        for i in range(pairs):
            rows = x_ref[pl.ds(i * modules + m, queries, stride=pairs * modules), :]
            o_ref[m * pairs + i] = rows.astype(jnp.bfloat16)


def token_kernel(modules, rank, x_ref, w_ref, a_ref, n_ref, wide):
    tokens = x_ref.shape[0] // modules
    wide[...] = x_ref[...].astype(jnp.float32)
    norm = jnp.zeros((1, tokens), jnp.float32)
    for m in range(modules):
        turned = wide[pl.ds(m, tokens, stride=modules), :].T
        act, grad = turned[:rank], turned[rank:]
        norm += jnp.sum(act * act, axis=0, keepdims=True) * jnp.sum(
            grad * grad, axis=0, keepdims=True
        )
        grad = grad.astype(jnp.bfloat16)
        w_ref[m, :rank] = grad
        w_ref[m, rank : 2 * rank] = jnp.zeros_like(grad)
        w_ref[m, 2 * rank :] = grad
        a_ref[m] = act
    n_ref[...] = jnp.broadcast_to(norm, n_ref.shape)


def score_kernel(count, modules, rank, *refs):
    blocks, w_ref, a_ref, o_ref = refs[:count], refs[count], refs[count + 1], refs[count + 2]
    tokens = w_ref.shape[2]
    pairs = rank // 2
    tile = 256 if tokens % 256 == 0 else tokens
    step = 8
    for b in range(count):
        total = jnp.zeros((GROUP, LANES), jnp.float32)
        for k in range(modules * pairs):
            v = blocks[b][k].astype(jnp.float32)
            total += v * v
        o_ref[b * GROUP : (b + 1) * GROUP, tokens:] = total

    @pl.loop(0, tokens // tile)
    def _(t):
        lanes = pl.ds(pl.multiple_of(t * tile, tile), tile)
        acc = [jnp.zeros((GROUP, tile), jnp.float32) for _ in range(count)]
        for m in range(modules):
            for odd in range(2):
                w = w_ref[m, odd * rank : (odd + 2) * rank, lanes]
                for b in range(count):
                    for i in range(0, pairs, step):
                        k = m * pairs + i
                        left = blocks[b][k : k + step].reshape(step * GROUP, LANES)
                        inner = jnp.dot(left, w, preferred_element_type=jnp.float32)
                        for s in range(step):
                            act = a_ref[m, pl.ds(2 * (i + s) + odd, 1), lanes]
                            acc[b] += inner[s * GROUP : (s + 1) * GROUP] * act
        for b in range(count):
            o_ref[b * GROUP : (b + 1) * GROUP, lanes] = acc[b]


def finish_kernel(count, width, slot_ref, *refs):
    own, far = refs[:count], refs[count : 2 * count]
    norm_ref, far_norm_ref, o_ref, both = refs[2 * count :]
    tokens = o_ref.shape[1]
    at = 0
    for mine, other in zip(own, far):
        rows = mine.shape[0]
        both[at : at + rows] = mine[...] + other[...]
        at += rows
    norm = norm_ref[:1] + far_norm_ref[:1]
    token_scale = lax.rsqrt(norm / width + epsilon) / jnp.sqrt(jnp.float32(width))
    for j in range(o_ref.shape[0] // GROUP):
        got = both[pl.ds(pl.multiple_of(slot_ref[j] * GROUP, GROUP), GROUP), :]
        square = jnp.sum(got[:, tokens:], axis=1, keepdims=True)
        query_scale = lax.rsqrt(square / width + epsilon)
        o_ref[j * GROUP : (j + 1) * GROUP] = got[:, :tokens] * query_scale * token_scale


def local(train_factors, query_grads):
    tokens, modules, doubled = train_factors.shape
    rank = doubled // 2
    pairs = rank // 2
    ex, proj = lax.axis_size("ex"), lax.axis_size("proj")
    here, core = lax.axis_index("ex"), lax.axis_index("proj")
    queries = query_grads.shape[0]
    width = modules * proj * rank * rank
    swap = [(i, (i + 1) % proj) for i in range(proj)]

    token_rows = train_factors.reshape(tokens * modules, doubled)
    weights, acts, norm = pl.pallas_call(
        functools.partial(token_kernel, modules, rank),
        out_shape=(
            jax.ShapeDtypeStruct((modules, 3 * rank, tokens), jnp.bfloat16),
            jax.ShapeDtypeStruct((modules, rank, tokens), jnp.float32),
            jax.ShapeDtypeStruct((8, tokens), jnp.float32),
        ),
        in_specs=[VMEM],
        out_specs=(VMEM, VMEM, VMEM),
        scratch_shapes=[pltpu.VMEM((tokens * modules, doubled), jnp.float32)],
        compiler_params=PARAMS,
        name="tokens",
    )(token_rows)

    def score(*blocks):
        count = len(blocks)
        flops = 2 * count * GROUP * modules * rank * rank * tokens
        return pl.pallas_call(
            functools.partial(score_kernel, count, modules, rank),
            out_shape=jax.ShapeDtypeStruct((count * GROUP, tokens + LANES), jnp.float32),
            in_specs=[VMEM] * (count + 2),
            out_specs=VMEM,
            compiler_params=PARAMS,
            cost_estimate=pl.CostEstimate(
                flops=4 * flops, bytes_accessed=2 * 1024 * 1024, transcendentals=0
            ),
            name="scores",
        )(*blocks, weights, acts)

    def swapped(x):
        return lax.ppermute(x, "proj", swap)

    if queries % GROUP == 0 and ex % 2 == 0 and ex <= 16 and queries == GROUP:
        order = list(range(0, ex, 2)) + list(range(ex - 1, 0, -2))
        up = [(order[i], order[(i + 1) % ex]) for i in range(ex)]
        down = [(b, a) for a, b in up]
        rows = query_grads.reshape(queries, modules, pairs, LANES)
        rows = rows.transpose(0, 2, 1, 3).reshape(queries * pairs * modules, LANES)
        block = pl.pallas_call(
            functools.partial(query_kernel, modules, pairs),
            out_shape=jax.ShapeDtypeStruct((modules * pairs, queries, LANES), jnp.bfloat16),
            in_specs=[VMEM],
            out_specs=VMEM,
            compiler_params=PARAMS,
            name="queries",
        )(rows)
        half = modules * pairs // 2
        low = high = block
        own, far = [], []
        waiting = (block,)
        for step in range(1, ex // 2 + 1):
            if step < ex // 2:
                low = lax.ppermute(low, "ex", up)
                high = lax.ppermute(high, "ex", down)
                arrived = (low, high)
            else:
                first = lax.ppermute(low[:half], "ex", up)
                second = lax.ppermute(high[half:], "ex", down)
                arrived = (jnp.concatenate([first, second], axis=0),)
            own.append(score(*waiting))
            far.append(swapped(own[-1]))
            waiting = arrived
        own.append(score(*waiting))
        far.append(swapped(own[-1]))
        place = jnp.array([order.index(i) for i in range(ex)], jnp.int32)
        wanted = core * (ex // proj) + jnp.arange(ex // proj, dtype=jnp.int32)
        ahead = jnp.mod(place[wanted] - place[here], ex)
        slots = jnp.where(
            ahead == 0,
            0,
            jnp.where(
                ahead < ex // 2,
                2 * ahead,
                jnp.where(ahead > ex // 2, 2 * (ex - ahead) - 1, ex - 1),
            ),
        )
    else:
        gathered = lax.all_gather(query_grads.astype(jnp.bfloat16), "ex", axis=0, tiled=True)
        count = queries * ex // GROUP
        gathered = gathered.reshape(count, GROUP, modules * pairs, LANES).transpose(0, 2, 1, 3)
        own = [score(gathered[i]) for i in range(count)]
        far = [swapped(x) for x in own]
        slots = core * (count // proj) + jnp.arange(count // proj, dtype=jnp.int32)

    count = len(own)
    total_rows = sum(x.shape[0] for x in own)
    scores = pl.pallas_call(
        functools.partial(finish_kernel, count, width),
        out_shape=jax.ShapeDtypeStruct((total_rows // proj, tokens), jnp.float32),
        in_specs=[pl.BlockSpec(memory_space=pltpu.SMEM)] + [VMEM] * (2 * count + 2),
        out_specs=VMEM,
        scratch_shapes=[pltpu.VMEM((total_rows, tokens + LANES), jnp.float32)],
        compiler_params=PARAMS,
        name="finish",
    )(slots.astype(jnp.int32), *own, *far, norm, swapped(norm))
    return scores.T


def solution(mesh):
    return jax.shard_map(
        local,
        mesh=mesh,
        in_specs=(P(("groups", "ex"), "proj", None), P(("groups", "ex"), "proj", None)),
        out_specs=P(("groups", "ex"), "proj"),
        check_vma=False,
    )
```

```python
import functools

import jax
import jax.numpy as jnp
from jax import lax
from jax.experimental import pallas as pl
from jax.experimental.pallas import tpu as pltpu
from jax.sharding import PartitionSpec as P

epsilon = 1e-06
LANES = 128
GROUP = 16
VMEM = pl.BlockSpec(memory_space=pltpu.VMEM)
ANY = pl.BlockSpec(memory_space=pl.ANY)
PARAMS = pltpu.CompilerParams(vmem_limit_bytes=16 * 1024 * 1024)


def place_of(index, count):
    return jnp.where(index % 2 == 0, index // 2, count - (index + 1) // 2)


def index_at(place, count):
    place = lax.rem(place + count, count)
    return jnp.where(place < count // 2, 2 * place, 2 * (count - place) - 1)


def query_kernel(modules, pairs, x_ref, *chunks):
    queries = chunks[0].shape[1]
    own = pairs // len(chunks)
    for c, o_ref in enumerate(chunks):
        for m in range(modules):
            for i in range(own):
                at = (c * own + i) * modules + m
                rows = x_ref[pl.ds(at, queries, stride=pairs * modules), :]
                o_ref[m * own + i] = rows.astype(jnp.bfloat16)


def token_kernel(modules, rank, x_ref, w_ref, a_ref, b_ref, n_ref, wide):
    tokens = x_ref.shape[0] // modules
    wide[...] = x_ref[...].astype(jnp.float32)
    norm = jnp.zeros((1, tokens), jnp.float32)
    for m in range(modules):
        turned = wide[pl.ds(m, tokens, stride=modules), :].T
        act, grad = turned[:rank], turned[rank:]
        norm += jnp.sum(act * act, axis=0, keepdims=True) * jnp.sum(
            grad * grad, axis=0, keepdims=True
        )
        grad = grad.astype(jnp.bfloat16)
        w_ref[m, :rank] = grad
        w_ref[m, rank : 2 * rank] = jnp.zeros_like(grad)
        w_ref[m, 2 * rank :] = grad
        a_ref[m] = act
        b_ref[m] = act.astype(jnp.bfloat16)
    n_ref[...] = jnp.broadcast_to(norm, n_ref.shape)


def lane_squares(chunks):
    total = jnp.zeros((GROUP, LANES), jnp.float32)
    for chunk in chunks:
        for k in range(chunk.shape[0]):
            v = chunk[k].astype(jnp.float32)
            total += v * v
    return total


def last_kernel(parts, modules, rank, *refs):
    chunks = refs[:parts]
    w_ref, a_ref, o_ref = refs[parts:]
    tokens = w_ref.shape[2]
    own = rank // 2 // parts
    step = min(8, own)
    tile = 512 if tokens % 512 == 0 else tokens
    o_ref[:, tokens:] = lane_squares(chunks)
    for t in range(0, tokens, tile):
        acc = jnp.zeros((GROUP, tile), jnp.float32)
        for m in range(modules):
            for odd in range(2):
                w = w_ref[m, odd * rank : (odd + 2) * rank, t : t + tile]
                for c, chunk in enumerate(chunks):
                    for i in range(0, own, step):
                        k = m * own + i
                        left = chunk[k : k + step].reshape(step * GROUP, LANES)
                        inner = jnp.dot(left, w, preferred_element_type=jnp.float32)
                        for s in range(step):
                            row = 2 * (c * own + i + s) + odd
                            acc += inner[s * GROUP : (s + 1) * GROUP] * a_ref[m, row : row + 1, t : t + tile]
        o_ref[:, t : t + tile] = acc


def bulk_kernel(count, parts, modules, rank, ring, core, *refs):
    blocks = [refs[b * parts : (b + 1) * parts] for b in range(count)]
    w_ref, b_ref, n_ref, keep_ref, send_ref, both = refs[count * parts :]
    tokens = w_ref.shape[2]
    own = rank // 2 // parts
    tile = 256 if tokens % 256 == 0 else tokens
    half = keep_ref.shape[0] // GROUP
    send_ref[half * GROUP :, :tokens] = n_ref[...]
    for b in range(count):
        both[b * GROUP : (b + 1) * GROUP, tokens:] = lane_squares(blocks[b])

    @pl.loop(0, tokens // tile)
    def _(t):
        lanes = pl.ds(pl.multiple_of(t * tile, tile), tile)
        acc = jnp.zeros((count * GROUP, tile), jnp.float32)
        for m in range(modules):
            grad = w_ref[m, :rank, lanes]
            for c in range(parts):
                for i in range(0, own, 2):
                    k = m * own + i
                    row = 2 * (c * own + i)
                    left = jnp.concatenate(
                        [
                            jnp.concatenate([blocks[b][c][k + s] for b in range(count)], axis=0)
                            for s in range(2)
                        ],
                        axis=1,
                    )
                    right = jnp.concatenate(
                        [grad * b_ref[m, row + s : row + s + 1, lanes] for s in range(4)], axis=0
                    )
                    acc += jnp.dot(left, right, preferred_element_type=jnp.float32)
        both[:, lanes] = acc

    me = lax.axis_index("proj") if core else 0
    for b, index in enumerate(ring()):
        rows = both[b * GROUP : (b + 1) * GROUP]
        at = pl.multiple_of(lax.rem(index, half) * GROUP, GROUP)

        @pl.when(index // half == me)
        def _():
            keep_ref[pl.ds(at, GROUP), :] = rows

        @pl.when(index // half != me)
        def _():
            send_ref[pl.ds(at, GROUP), :] = rows


def scaled(rows, tokens, width, token_scale):
    square = jnp.sum(rows[:, tokens:], axis=1, keepdims=True)
    return rows[:, :tokens] * lax.rsqrt(square / width + epsilon) * token_scale


def most_kernel(width, keep_ref, far_ref, n_ref, o_ref, s_ref):
    rows, tokens = o_ref.shape
    norm = n_ref[...] + far_ref[rows:, :tokens]
    scale = lax.rsqrt(norm / width + epsilon) / jnp.sqrt(jnp.float32(width))
    s_ref[...] = scale
    o_ref[...] = scaled(keep_ref[...] + far_ref[:rows], tokens, width, scale[:1])


def rest_kernel(width, ring, own_ref, far_ref, s_ref, most_ref, o_ref, rows, sem):
    del most_ref
    tokens = o_ref.shape[1]
    half = o_ref.shape[0] // GROUP
    index = ring()

    @pl.when(index // half == lax.axis_index("proj"))
    def _():
        rows[...] = scaled(own_ref[...] + far_ref[...], tokens, width, s_ref[:1])
        at = pl.multiple_of(lax.rem(index, half) * GROUP, GROUP)
        copy = pltpu.make_async_copy(rows, o_ref.at[pl.ds(at, GROUP), :], sem)
        copy.start()
        copy.wait()


def local(train_factors, query_grads):
    tokens, modules, doubled = train_factors.shape
    rank = doubled // 2
    pairs = rank // 2
    ex, proj = lax.axis_size("ex"), lax.axis_size("proj")
    queries = query_grads.shape[0]
    width = modules * proj * rank * rank
    wide = tokens + LANES
    columns = queries * ex // proj

    token_rows = train_factors.reshape(tokens * modules, doubled)
    weights, acts, narrow, norm = pl.pallas_call(
        functools.partial(token_kernel, modules, rank),
        out_shape=(
            jax.ShapeDtypeStruct((modules, 3 * rank, tokens), jnp.bfloat16),
            jax.ShapeDtypeStruct((modules, rank, tokens), jnp.float32),
            jax.ShapeDtypeStruct((modules, rank, tokens), jnp.bfloat16),
            jax.ShapeDtypeStruct((8, tokens), jnp.float32),
        ),
        in_specs=[VMEM],
        out_specs=(VMEM,) * 4,
        scratch_shapes=[pltpu.VMEM((tokens * modules, doubled), jnp.float32)],
        compiler_params=PARAMS,
        name="tokens",
    )(token_rows)

    def swapped(x):
        return lax.ppermute(x, "proj", [(i, (i + 1) % proj) for i in range(proj)])

    def bulk(blocks, ring):
        count, parts = len(blocks), len(blocks[0])
        return pl.pallas_call(
            functools.partial(bulk_kernel, count, parts, modules, rank, ring, proj > 1),
            out_shape=(
                jax.ShapeDtypeStruct((columns, wide), jnp.float32),
                jax.ShapeDtypeStruct((columns + 8, wide), jnp.float32),
            ),
            in_specs=[VMEM] * (count * parts + 3),
            out_specs=(VMEM, VMEM),
            scratch_shapes=[pltpu.VMEM((count * GROUP, wide), jnp.float32)],
            compiler_params=PARAMS,
            cost_estimate=pl.CostEstimate(
                flops=4 * 2 * 128 * modules * rank * rank * tokens,
                bytes_accessed=4 * 1024 * 1024,
                transcendentals=0,
            ),
            name="bulk",
        )(*[chunk for block in blocks for chunk in block], weights, narrow, norm)

    def most(keep, far):
        return pl.pallas_call(
            functools.partial(most_kernel, width),
            out_shape=(
                jax.ShapeDtypeStruct((columns, tokens), jnp.float32),
                jax.ShapeDtypeStruct((8, tokens), jnp.float32),
            ),
            in_specs=[VMEM] * 3,
            out_specs=(VMEM, VMEM),
            compiler_params=PARAMS,
            name="most",
        )(keep, far, norm)

    if queries == GROUP and ex % 2 == 0 and ex <= 16:
        order = list(range(0, ex, 2)) + list(range(ex - 1, 0, -2))
        up_pairs = [(order[i], order[(i + 1) % ex]) for i in range(ex)]
        down_pairs = [(b, a) for a, b in up_pairs]

        def up(x):
            return lax.ppermute(x, "ex", up_pairs)

        def down(x):
            return lax.ppermute(x, "ex", down_pairs)

        rows = query_grads.reshape(queries, modules, pairs, LANES)
        rows = rows.transpose(0, 2, 1, 3).reshape(queries * pairs * modules, LANES)
        chunk = jax.ShapeDtypeStruct((modules * pairs // 2, queries, LANES), jnp.bfloat16)
        block = pl.pallas_call(
            functools.partial(query_kernel, modules, pairs),
            out_shape=(chunk, chunk),
            in_specs=[VMEM],
            out_specs=(VMEM, VMEM),
            compiler_params=PARAMS,
            name="queries",
        )(rows)
        below, above = block, block
        blocks, steps = [block], [0]
        for step in range(1, ex // 2):
            first = (up(below[0]), down(above[0]))
            second = (up(below[1]), down(above[1]))
            below, above = (first[0], second[0]), (first[1], second[1])
            blocks += [below, above]
            steps += [-step, step]
        across = (up(below[0]), down(above[1]))

        def ring():
            here = place_of(lax.axis_index("ex"), ex)
            return [index_at(here + step, ex) for step in steps]

        def opposite():
            return index_at(place_of(lax.axis_index("ex"), ex) + ex // 2, ex)

        keep, send = bulk(blocks, ring)
        out, scale = most(keep, swapped(send))
        mine = pl.pallas_call(
            functools.partial(last_kernel, 2, modules, rank),
            out_shape=jax.ShapeDtypeStruct((GROUP, wide), jnp.float32),
            in_specs=[VMEM] * 4,
            out_specs=VMEM,
            compiler_params=PARAMS,
            name="last",
        )(*across, weights, acts)
        out = pl.pallas_call(
            functools.partial(rest_kernel, width, opposite),
            out_shape=jax.ShapeDtypeStruct((columns, tokens), jnp.float32),
            in_specs=[VMEM, VMEM, VMEM, ANY],
            out_specs=ANY,
            scratch_shapes=[pltpu.VMEM((GROUP, tokens), jnp.float32), pltpu.SemaphoreType.DMA],
            input_output_aliases={3: 0},
            compiler_params=PARAMS,
            name="rest",
        )(mine, swapped(mine), scale, out)
    else:
        gathered = lax.all_gather(query_grads.astype(jnp.bfloat16), "ex", axis=0, tiled=True)
        count = queries * ex // GROUP
        gathered = gathered.reshape(count, GROUP, modules * pairs, LANES).transpose(0, 2, 1, 3)
        blocks = [(gathered[i],) for i in range(count)]
        keep, send = bulk(blocks, lambda: [jnp.int32(i) for i in range(count)])
        out, _ = most(keep, swapped(send))
    return out.T


def solution(mesh):
    return jax.shard_map(
        local,
        mesh=mesh,
        in_specs=(P(("groups", "ex"), "proj", None), P(("groups", "ex"), "proj", None)),
        out_specs=P(("groups", "ex"), "proj"),
        check_vma=False,
    )
```

```python
import functools

import jax
import jax.numpy as jnp
from jax import lax
from jax.experimental import pallas as pl
from jax.experimental.pallas import tpu as pltpu
from jax.sharding import PartitionSpec as P

epsilon = 1e-06
LANES = 128
GROUP = 16
VMEM = pl.BlockSpec(memory_space=pltpu.VMEM)
ANY = pl.BlockSpec(memory_space=pl.ANY)
PARAMS = pltpu.CompilerParams(vmem_limit_bytes=16 * 1024 * 1024)
LONG = pl.CostEstimate(flops=10**10, bytes_accessed=4 * 1024 * 1024, transcendentals=0)


def place_of(index, count):
    return jnp.where(index % 2 == 0, index // 2, count - (index + 1) // 2)


def index_at(place, count):
    place = lax.rem(place + count, count)
    return jnp.where(place < count // 2, 2 * place, 2 * (count - place) - 1)


def query_kernel(modules, pairs, x_ref, *chunks):
    queries = chunks[0].shape[1]
    own = pairs // len(chunks)
    for c, o_ref in enumerate(chunks):
        for m in range(modules):
            for i in range(own):
                at = (c * own + i) * modules + m
                rows = x_ref[pl.ds(at, queries, stride=pairs * modules), :]
                o_ref[m * own + i] = rows.astype(jnp.bfloat16)


def token_kernel(modules, rank, x_ref, w_ref, a_ref, b_ref, n_ref, wide):
    tokens = x_ref.shape[0] // modules
    wide[...] = x_ref[...].astype(jnp.float32)
    norm = jnp.zeros((1, tokens), jnp.float32)
    for m in range(modules):
        turned = wide[pl.ds(m, tokens, stride=modules), :].T
        act, grad = turned[:rank], turned[rank:]
        norm += jnp.sum(act * act, axis=0, keepdims=True) * jnp.sum(
            grad * grad, axis=0, keepdims=True
        )
        grad = grad.astype(jnp.bfloat16)
        w_ref[m, :rank] = grad
        w_ref[m, rank : 2 * rank] = jnp.zeros_like(grad)
        w_ref[m, 2 * rank :] = grad
        a_ref[m] = act
        b_ref[m] = act.astype(jnp.bfloat16)
    n_ref[...] = jnp.broadcast_to(norm, n_ref.shape)


def lane_squares(chunks):
    total = jnp.zeros((GROUP, LANES), jnp.float32)
    for chunk in chunks:
        for k in range(chunk.shape[0]):
            v = chunk[k].astype(jnp.float32)
            total += v * v
    return total


def last_kernel(parts, modules, rank, *refs):
    chunks = refs[:parts]
    w_ref, a_ref, o_ref = refs[parts:]
    tokens = w_ref.shape[2]
    own = rank // 2 // parts
    step = min(8, own)
    tile = 512 if tokens % 512 == 0 else tokens
    o_ref[:, tokens:] = lane_squares(chunks)
    for t in range(0, tokens, tile):
        acc = jnp.zeros((GROUP, tile), jnp.float32)
        for m in range(modules):
            for odd in range(2):
                w = w_ref[m, odd * rank : (odd + 2) * rank, t : t + tile]
                for c, chunk in enumerate(chunks):
                    for i in range(0, own, step):
                        k = m * own + i
                        left = chunk[k : k + step].reshape(step * GROUP, LANES)
                        inner = jnp.dot(left, w, preferred_element_type=jnp.float32)
                        for s in range(step):
                            row = 2 * (c * own + i + s) + odd
                            acc += inner[s * GROUP : (s + 1) * GROUP] * a_ref[m, row : row + 1, t : t + tile]
        o_ref[:, t : t + tile] = acc


def products(blocks, part, parts, modules, rank, w_ref, b_ref, lanes):
    own = rank // 2 // parts
    acc = jnp.zeros((len(blocks) * GROUP, lanes.size), jnp.float32)
    for m in range(modules):
        grad = w_ref[m, :rank, lanes]
        for i in range(0, own, 2):
            k = m * own + i
            row = 2 * (part * own + i)
            left = jnp.concatenate(
                [jnp.concatenate([block[k + s] for block in blocks], axis=0) for s in range(2)],
                axis=1,
            )
            right = jnp.concatenate(
                [grad * b_ref[m, row + s : row + s + 1, lanes] for s in range(4)], axis=0
            )
            acc += jnp.dot(left, right, preferred_element_type=jnp.float32)
    return acc


def early_kernel(count, parts, modules, rank, *refs):
    blocks = refs[:count]
    w_ref, b_ref, o_ref = refs[count:]
    tokens = w_ref.shape[2]
    tile = 256 if tokens % 256 == 0 else tokens
    for b in range(count):
        o_ref[b * GROUP : (b + 1) * GROUP, tokens:] = lane_squares(blocks[b : b + 1])

    @pl.loop(0, tokens // tile)
    def _(t):
        lanes = pl.ds(pl.multiple_of(t * tile, tile), tile)
        o_ref[:, lanes] = products(blocks, parts - 1, parts, modules, rank, w_ref, b_ref, lanes)


def late_kernel(count, parts, modules, rank, ring, *refs):
    blocks = refs[:count]
    w_ref, b_ref, n_ref, sum_ref, keep_ref, send_ref, both = refs[count:]
    tokens = w_ref.shape[2]
    tile = 256 if tokens % 256 == 0 else tokens
    half = keep_ref.shape[0] // GROUP
    send_ref[half * GROUP :, :tokens] = n_ref[...]
    for b in range(count):
        span = slice(b * GROUP, (b + 1) * GROUP)
        both[span, tokens:] = sum_ref[span, tokens:] + lane_squares(blocks[b : b + 1])

    @pl.loop(0, tokens // tile)
    def _(t):
        lanes = pl.ds(pl.multiple_of(t * tile, tile), tile)
        both[:, lanes] = sum_ref[:, lanes] + products(
            blocks, 0, parts, modules, rank, w_ref, b_ref, lanes
        )

    me = lax.axis_index("proj")
    for b, index in enumerate(ring()):
        rows = both[b * GROUP : (b + 1) * GROUP]
        at = pl.multiple_of(lax.rem(index, half) * GROUP, GROUP)

        @pl.when(index // half == me)
        def _():
            keep_ref[pl.ds(at, GROUP), :] = rows

        @pl.when(index // half != me)
        def _():
            send_ref[pl.ds(at, GROUP), :] = rows


def scaled(rows, tokens, width, token_scale):
    square = jnp.sum(rows[:, tokens:], axis=1, keepdims=True)
    return rows[:, :tokens] * lax.rsqrt(square / width + epsilon) * token_scale


def most_kernel(width, keep_ref, far_ref, n_ref, o_ref, s_ref):
    rows, tokens = o_ref.shape
    norm = n_ref[...] + far_ref[rows:, :tokens]
    scale = lax.rsqrt(norm / width + epsilon) / jnp.sqrt(jnp.float32(width))
    s_ref[...] = scale
    o_ref[...] = scaled(keep_ref[...] + far_ref[:rows], tokens, width, scale[:1])


def rest_kernel(width, ring, own_ref, far_ref, s_ref, most_ref, o_ref, rows, sem):
    del most_ref
    tokens = o_ref.shape[1]
    half = o_ref.shape[0] // GROUP
    index = ring()

    @pl.when(index // half == lax.axis_index("proj"))
    def _():
        rows[...] = scaled(own_ref[...] + far_ref[...], tokens, width, s_ref[:1])
        at = pl.multiple_of(lax.rem(index, half) * GROUP, GROUP)
        copy = pltpu.make_async_copy(rows, o_ref.at[pl.ds(at, GROUP), :], sem)
        copy.start()
        copy.wait()


def local(train_factors, query_grads):
    tokens, modules, doubled = train_factors.shape
    rank = doubled // 2
    pairs = rank // 2
    ex, proj = lax.axis_size("ex"), lax.axis_size("proj")
    queries = query_grads.shape[0]
    width = modules * proj * rank * rank
    wide = tokens + LANES
    columns = queries * ex // proj

    token_rows = train_factors.reshape(tokens * modules, doubled)
    weights, acts, narrow, norm = pl.pallas_call(
        functools.partial(token_kernel, modules, rank),
        out_shape=(
            jax.ShapeDtypeStruct((modules, 3 * rank, tokens), jnp.bfloat16),
            jax.ShapeDtypeStruct((modules, rank, tokens), jnp.float32),
            jax.ShapeDtypeStruct((modules, rank, tokens), jnp.bfloat16),
            jax.ShapeDtypeStruct((8, tokens), jnp.float32),
        ),
        in_specs=[VMEM],
        out_specs=(VMEM,) * 4,
        scratch_shapes=[pltpu.VMEM((tokens * modules, doubled), jnp.float32)],
        compiler_params=PARAMS,
        name="tokens",
    )(token_rows)

    def swapped(x):
        return lax.ppermute(x, "proj", [(i, (i + 1) % proj) for i in range(proj)])

    def bulk(blocks, ring):
        count, parts = len(blocks), len(blocks[0])
        early = pl.pallas_call(
            functools.partial(early_kernel, count, parts, modules, rank),
            out_shape=jax.ShapeDtypeStruct((count * GROUP, wide), jnp.float32),
            in_specs=[VMEM] * (count + 2),
            out_specs=VMEM,
            compiler_params=PARAMS,
            cost_estimate=LONG,
            name="early",
        )(*[block[-1] for block in blocks], weights, narrow)
        return pl.pallas_call(
            functools.partial(late_kernel, count, parts, modules, rank, ring),
            out_shape=(
                jax.ShapeDtypeStruct((columns, wide), jnp.float32),
                jax.ShapeDtypeStruct((columns + 8, wide), jnp.float32),
            ),
            in_specs=[VMEM] * (count + 4),
            out_specs=(VMEM, VMEM),
            scratch_shapes=[pltpu.VMEM((count * GROUP, wide), jnp.float32)],
            compiler_params=PARAMS,
            cost_estimate=LONG,
            name="late",
        )(*[block[0] for block in blocks], weights, narrow, norm, early)

    def most(keep, far):
        return pl.pallas_call(
            functools.partial(most_kernel, width),
            out_shape=(
                jax.ShapeDtypeStruct((columns, tokens), jnp.float32),
                jax.ShapeDtypeStruct((8, tokens), jnp.float32),
            ),
            in_specs=[VMEM] * 3,
            out_specs=(VMEM, VMEM),
            compiler_params=PARAMS,
            cost_estimate=LONG,
            name="most",
        )(keep, far, norm)

    if queries == GROUP and ex % 2 == 0 and ex <= 16:
        order = list(range(0, ex, 2)) + list(range(ex - 1, 0, -2))
        up_pairs = [(order[i], order[(i + 1) % ex]) for i in range(ex)]
        down_pairs = [(b, a) for a, b in up_pairs]

        def up(x):
            return lax.ppermute(x, "ex", up_pairs)

        def down(x):
            return lax.ppermute(x, "ex", down_pairs)

        rows = query_grads.reshape(queries, modules, pairs, LANES)
        rows = rows.transpose(0, 2, 1, 3).reshape(queries * pairs * modules, LANES)
        chunk = jax.ShapeDtypeStruct((modules * pairs // 2, queries, LANES), jnp.bfloat16)
        block = pl.pallas_call(
            functools.partial(query_kernel, modules, pairs),
            out_shape=(chunk, chunk),
            in_specs=[VMEM],
            out_specs=(VMEM, VMEM),
            compiler_params=PARAMS,
            name="queries",
        )(rows)
        below, above = block, block
        blocks, steps = [block], [0]
        for step in range(1, ex // 2):
            first = (up(below[0]), down(above[0]))
            second = (up(below[1]), down(above[1]))
            below, above = (first[0], second[0]), (first[1], second[1])
            blocks += [below, above]
            steps += [-step, step]
        across = (up(below[0]), down(above[1]))

        def ring():
            here = place_of(lax.axis_index("ex"), ex)
            return [index_at(here + step, ex) for step in steps]

        def opposite():
            return index_at(place_of(lax.axis_index("ex"), ex) + ex // 2, ex)

        keep, send = bulk(blocks, ring)
        out, scale = most(keep, swapped(send))
        mine = pl.pallas_call(
            functools.partial(last_kernel, 2, modules, rank),
            out_shape=jax.ShapeDtypeStruct((GROUP, wide), jnp.float32),
            in_specs=[VMEM] * 4,
            out_specs=VMEM,
            compiler_params=PARAMS,
            cost_estimate=LONG,
            name="last",
        )(*across, weights, acts)
        out = pl.pallas_call(
            functools.partial(rest_kernel, width, opposite),
            out_shape=jax.ShapeDtypeStruct((columns, tokens), jnp.float32),
            in_specs=[VMEM, VMEM, VMEM, ANY],
            out_specs=ANY,
            scratch_shapes=[pltpu.VMEM((GROUP, tokens), jnp.float32), pltpu.SemaphoreType.DMA],
            input_output_aliases={3: 0},
            compiler_params=PARAMS,
            name="rest",
        )(mine, swapped(mine), scale, out)
    else:
        gathered = lax.all_gather(query_grads.astype(jnp.bfloat16), "ex", axis=0, tiled=True)
        count = queries * ex // GROUP
        gathered = gathered.reshape(count, GROUP, modules, 2, pairs // 2, LANES)
        gathered = gathered.transpose(0, 3, 2, 4, 1, 5).reshape(count, 2, -1, GROUP, LANES)
        blocks = [(gathered[i, 0], gathered[i, 1]) for i in range(count)]
        keep, send = bulk(blocks, lambda: [jnp.int32(i) for i in range(count)])
        out, _ = most(keep, swapped(send))
    return out.T


def solution(mesh):
    return jax.shard_map(
        local,
        mesh=mesh,
        in_specs=(P(("groups", "ex"), "proj", None), P(("groups", "ex"), "proj", None)),
        out_specs=P(("groups", "ex"), "proj"),
        check_vma=False,
    )
```

```python
import functools

import jax
import jax.numpy as jnp
from jax import lax
from jax.experimental import pallas as pl
from jax.experimental.pallas import tpu as pltpu
from jax.sharding import PartitionSpec as P

epsilon = 1e-06
LANES = 128
GROUP = 16
VMEM = pl.BlockSpec(memory_space=pltpu.VMEM)
HBM = pl.BlockSpec(memory_space=pltpu.HBM)
ANY = pl.BlockSpec(memory_space=pl.ANY)
PARAMS = pltpu.CompilerParams(vmem_limit_bytes=16 * 1024 * 1024)
LONG = pl.CostEstimate(flops=10**10, bytes_accessed=4 * 1024 * 1024, transcendentals=0)


def place_of(index, count):
    return lax.rem(count - jnp.where(index % 2 == 0, index // 2, count - (index + 1) // 2), count)


def index_at(place, count):
    place = lax.rem(2 * count - place, count)
    return jnp.where(place < count // 2, 2 * place, 2 * (count - place) - 1)


def query_kernel(modules, pairs, x_ref, *refs):
    chunks, rows, sems = refs[:-2], refs[-2], refs[-1]
    queries = chunks[0].shape[1]
    own = pairs // len(chunks)
    span = own * modules
    copies = [
        pltpu.make_async_copy(x_ref.at[:, pl.ds(c * span, span), :], rows.at[c], sems.at[c])
        for c in range(len(chunks))
    ]
    for copy in copies:
        copy.start()
    for c, o_ref in enumerate(chunks):
        copies[c].wait()
        flat = rows.at[c].reshape(queries * span, LANES)
        for m in range(modules):
            for i in range(own):
                got = flat[pl.ds(i * modules + m, queries, stride=span), :]
                o_ref[m * own + i] = got.astype(jnp.bfloat16)


def token_kernel(modules, rank, x_ref, w_ref, a_ref, b_ref, n_ref, rows, wide, sem):
    tokens = x_ref.shape[0] // modules
    copy = pltpu.make_async_copy(x_ref, rows, sem)
    copy.start()
    copy.wait()
    wide[...] = rows[...].astype(jnp.float32)
    norm = jnp.zeros((1, tokens), jnp.float32)
    for m in range(modules):
        turned = wide[pl.ds(m, tokens, stride=modules), :].T
        act, grad = turned[:rank], turned[rank:]
        norm += jnp.sum(act * act, axis=0, keepdims=True) * jnp.sum(
            grad * grad, axis=0, keepdims=True
        )
        grad = grad.astype(jnp.bfloat16)
        w_ref[m, :rank] = grad
        w_ref[m, rank : 2 * rank] = jnp.zeros_like(grad)
        w_ref[m, 2 * rank :] = grad
        a_ref[m] = act
        b_ref[m] = act.astype(jnp.bfloat16)
    n_ref[...] = jnp.broadcast_to(norm, n_ref.shape)


def lane_squares(chunks):
    total = jnp.zeros((GROUP, LANES), jnp.float32)
    for chunk in chunks:
        for k in range(chunk.shape[0]):
            v = chunk[k].astype(jnp.float32)
            total += v * v
    return total


def last_kernel(parts, modules, rank, *refs):
    chunks = refs[:parts]
    w_ref, a_ref, o_ref = refs[parts:]
    tokens = w_ref.shape[2]
    own = rank // 2 // parts
    step = min(8, own)
    o_ref[:, tokens:] = lane_squares(chunks)
    for lanes in tiles(tokens):
        acc = jnp.zeros((GROUP, lanes.stop - lanes.start), jnp.float32)
        for m in range(modules):
            for odd in range(2):
                w = w_ref[m, odd * rank : (odd + 2) * rank, lanes]
                for part, chunk in enumerate(chunks):
                    for i in range(0, own, step):
                        k = m * own + i
                        left = chunk[k : k + step].reshape(step * GROUP, LANES)
                        inner = jnp.dot(left, w, preferred_element_type=jnp.float32)
                        for s in range(step):
                            row = 2 * (part * own + i + s) + odd
                            acc += inner[s * GROUP : (s + 1) * GROUP] * a_ref[m, row : row + 1, lanes]
        o_ref[:, lanes] = acc


def products(blocks, part, parts, modules, rank, w_ref, b_ref, lanes):
    own = rank // 2 // parts
    step = min(4, own)
    acc = jnp.zeros((len(blocks) * GROUP, lanes.stop - lanes.start), jnp.float32)
    for m in range(modules):
        grad = w_ref[m, :rank, lanes]
        for i in range(0, own, step):
            k = m * own + i
            row = 2 * (part * own + i)
            left = jnp.concatenate(
                [jnp.concatenate([block[k + s] for block in blocks], axis=0) for s in range(step)],
                axis=1,
            )
            right = jnp.concatenate(
                [grad * b_ref[m, row + s : row + s + 1, lanes] for s in range(2 * step)], axis=0
            )
            acc += jnp.dot(left, right, preferred_element_type=jnp.float32)
    return acc


def tiles(tokens):
    size = 512 if tokens % 512 == 0 else tokens
    return [slice(t, t + size) for t in range(0, tokens, size)]


def early_kernel(count, parts, modules, rank, *refs):
    blocks = refs[:count]
    w_ref, b_ref, o_ref = refs[count:]
    tokens = w_ref.shape[2]
    for b in range(count):
        o_ref[b * GROUP : (b + 1) * GROUP, tokens:] = lane_squares(blocks[b : b + 1])

    for lanes in tiles(tokens):
        o_ref[:, lanes] = products(blocks, parts - 1, parts, modules, rank, w_ref, b_ref, lanes)


def late_kernel(count, parts, modules, rank, ring, *refs):
    blocks = refs[:count]
    w_ref, b_ref, n_ref, sum_ref, keep_ref, send_ref, both = refs[count:]
    tokens = w_ref.shape[2]
    half = keep_ref.shape[0] // GROUP
    send_ref[half * GROUP :, :tokens] = n_ref[...]
    for b in range(count):
        span = slice(b * GROUP, (b + 1) * GROUP)
        both[span, tokens:] = sum_ref[span, tokens:] + lane_squares(blocks[b : b + 1])

    for lanes in tiles(tokens):
        both[:, lanes] = sum_ref[:, lanes] + products(
            blocks, 0, parts, modules, rank, w_ref, b_ref, lanes
        )

    me = lax.axis_index("proj")
    for b, index in enumerate(ring()):
        rows = both[b * GROUP : (b + 1) * GROUP]
        at = pl.multiple_of(lax.rem(index, half) * GROUP, GROUP)

        @pl.when(index // half == me)
        def _():
            keep_ref[pl.ds(at, GROUP), :] = rows

        @pl.when(index // half != me)
        def _():
            send_ref[pl.ds(at, GROUP), :] = rows


def scaled(rows, tokens, width, token_scale):
    square = jnp.sum(rows[:, tokens:], axis=1, keepdims=True)
    return rows[:, :tokens] * lax.rsqrt(square / width + epsilon) * token_scale


def most_kernel(width, keep_ref, far_ref, n_ref, o_ref, s_ref):
    rows, tokens = o_ref.shape
    norm = n_ref[...] + far_ref[rows:, :tokens]
    scale = lax.rsqrt(norm / width + epsilon) / jnp.sqrt(jnp.float32(width))
    s_ref[...] = scale
    o_ref[...] = scaled(keep_ref[...] + far_ref[:rows], tokens, width, scale[:1])


def rest_kernel(width, ring, own_ref, far_ref, s_ref, most_ref, o_ref, rows, sem):
    del most_ref
    tokens = o_ref.shape[1]
    half = o_ref.shape[0] // GROUP
    index = ring()

    @pl.when(index // half == lax.axis_index("proj"))
    def _():
        rows[...] = scaled(own_ref[...] + far_ref[...], tokens, width, s_ref[:1])
        at = pl.multiple_of(lax.rem(index, half) * GROUP, GROUP)
        copy = pltpu.make_async_copy(rows, o_ref.at[pl.ds(at, GROUP), :], sem)
        copy.start()
        copy.wait()


def local(train_factors, query_grads):
    tokens, modules, doubled = train_factors.shape
    rank = doubled // 2
    pairs = rank // 2
    ex, proj = lax.axis_size("ex"), lax.axis_size("proj")
    queries = query_grads.shape[0]
    width = modules * proj * rank * rank
    wide = tokens + LANES
    columns = queries * ex // proj

    token_rows = train_factors.reshape(tokens * modules, doubled)
    weights, acts, narrow, norm = pl.pallas_call(
        functools.partial(token_kernel, modules, rank),
        out_shape=(
            jax.ShapeDtypeStruct((modules, 3 * rank, tokens), jnp.bfloat16),
            jax.ShapeDtypeStruct((modules, rank, tokens), jnp.float32),
            jax.ShapeDtypeStruct((modules, rank, tokens), jnp.bfloat16),
            jax.ShapeDtypeStruct((8, tokens), jnp.float32),
        ),
        in_specs=[HBM],
        out_specs=(VMEM,) * 4,
        scratch_shapes=[
            pltpu.VMEM((tokens * modules, doubled), jnp.bfloat16),
            pltpu.VMEM((tokens * modules, doubled), jnp.float32),
            pltpu.SemaphoreType.DMA,
        ],
        compiler_params=PARAMS,
        name="tokens",
    )(pltpu.with_memory_space_constraint(token_rows, pltpu.HBM))

    def swapped(x):
        return lax.ppermute(x, "proj", [(i, (i + 1) % proj) for i in range(proj)])

    def bulk(blocks, ring):
        count, parts = len(blocks), len(blocks[0])
        early = pl.pallas_call(
            functools.partial(early_kernel, count, parts, modules, rank),
            out_shape=jax.ShapeDtypeStruct((count * GROUP, wide), jnp.float32),
            in_specs=[VMEM] * (count + 2),
            out_specs=VMEM,
            compiler_params=PARAMS,
            cost_estimate=LONG,
            name="early",
        )(*[block[-1] for block in blocks], weights, narrow)
        return pl.pallas_call(
            functools.partial(late_kernel, count, parts, modules, rank, ring),
            out_shape=(
                jax.ShapeDtypeStruct((columns, wide), jnp.float32),
                jax.ShapeDtypeStruct((columns + 8, wide), jnp.float32),
            ),
            in_specs=[VMEM] * (count + 4),
            out_specs=(VMEM, VMEM),
            scratch_shapes=[pltpu.VMEM((count * GROUP, wide), jnp.float32)],
            compiler_params=PARAMS,
            cost_estimate=LONG,
            name="late",
        )(*[block[0] for block in blocks], weights, narrow, norm, early)

    def most(keep, far):
        return pl.pallas_call(
            functools.partial(most_kernel, width),
            out_shape=(
                jax.ShapeDtypeStruct((columns, tokens), jnp.float32),
                jax.ShapeDtypeStruct((8, tokens), jnp.float32),
            ),
            in_specs=[VMEM] * 3,
            out_specs=(VMEM, VMEM),
            compiler_params=PARAMS,
            cost_estimate=LONG,
            name="most",
        )(keep, far, norm)

    if queries == GROUP and ex % 2 == 0 and ex <= 16:
        order = list(range(0, ex, 2)) + list(range(ex - 1, 0, -2))
        order = order[:1] + order[:0:-1]
        up_pairs = [(order[i], order[(i + 1) % ex]) for i in range(ex)]
        down_pairs = [(b, a) for a, b in up_pairs]

        def up(x):
            return lax.ppermute(x, "ex", up_pairs)

        def down(x):
            return lax.ppermute(x, "ex", down_pairs)

        rows = query_grads.reshape(queries, modules, pairs, LANES)
        rows = rows.transpose(0, 2, 1, 3).reshape(queries, pairs * modules, LANES)
        chunk = jax.ShapeDtypeStruct((modules * pairs // 2, queries, LANES), jnp.bfloat16)
        block = pl.pallas_call(
            functools.partial(query_kernel, modules, pairs),
            out_shape=(chunk, chunk),
            in_specs=[HBM],
            out_specs=(VMEM, VMEM),
            scratch_shapes=[
                pltpu.VMEM((2, queries, pairs * modules // 2, LANES), jnp.float32),
                pltpu.SemaphoreType.DMA((2,)),
            ],
            compiler_params=PARAMS,
            name="queries",
        )(pltpu.with_memory_space_constraint(rows, pltpu.HBM))
        below, above = block, block
        blocks, steps = [block], [0]
        for step in range(1, ex // 2):
            first = (up(below[0]), down(above[0]))
            second = (up(below[1]), down(above[1]))
            if step == 1:
                arrived, weights = lax.optimization_barrier((first[0], weights))
                first = (arrived, first[1])
            below, above = (first[0], second[0]), (first[1], second[1])
            blocks += [below, above]
            steps += [-step, step]
        across = (up(below[0]), down(above[1]))

        def ring():
            here = place_of(lax.axis_index("ex"), ex)
            return [index_at(here + step, ex) for step in steps]

        def opposite():
            return index_at(place_of(lax.axis_index("ex"), ex) + ex // 2, ex)

        keep, send = bulk(blocks, ring)
        out, scale = most(keep, swapped(send))
        mine = pl.pallas_call(
            functools.partial(last_kernel, len(across), modules, rank),
            out_shape=jax.ShapeDtypeStruct((GROUP, wide), jnp.float32),
            in_specs=[VMEM] * (len(across) + 2),
            out_specs=VMEM,
            compiler_params=PARAMS,
            cost_estimate=LONG,
            name="last",
        )(*across, weights, acts)
        out = pl.pallas_call(
            functools.partial(rest_kernel, width, opposite),
            out_shape=jax.ShapeDtypeStruct((columns, tokens), jnp.float32),
            in_specs=[VMEM, VMEM, VMEM, ANY],
            out_specs=ANY,
            scratch_shapes=[pltpu.VMEM((GROUP, tokens), jnp.float32), pltpu.SemaphoreType.DMA],
            input_output_aliases={3: 0},
            compiler_params=PARAMS,
            name="rest",
        )(mine, swapped(mine), scale, out)
    else:
        gathered = lax.all_gather(query_grads.astype(jnp.bfloat16), "ex", axis=0, tiled=True)
        count = queries * ex // GROUP
        gathered = gathered.reshape(count, GROUP, modules, 2, pairs // 2, LANES)
        gathered = gathered.transpose(0, 3, 2, 4, 1, 5).reshape(count, 2, -1, GROUP, LANES)
        blocks = [(gathered[i, 0], gathered[i, 1]) for i in range(count)]
        keep, send = bulk(blocks, lambda: [jnp.int32(i) for i in range(count)])
        out, _ = most(keep, swapped(send))
    return out.T


def solution(mesh):
    return jax.shard_map(
        local,
        mesh=mesh,
        in_specs=(P(("groups", "ex"), "proj", None), P(("groups", "ex"), "proj", None)),
        out_specs=P(("groups", "ex"), "proj"),
        check_vma=False,
    )
```

```python
import functools

import jax
import jax.numpy as jnp
from jax import lax
from jax.experimental import pallas as pl
from jax.experimental.pallas import tpu as pltpu
from jax.sharding import PartitionSpec as P

epsilon = 1e-06
LANES = 128
GROUP = 16
VMEM = pl.BlockSpec(memory_space=pltpu.VMEM)
HBM = pl.BlockSpec(memory_space=pltpu.HBM)
COVER = pl.CostEstimate(flops=692100000, bytes_accessed=1024, transcendentals=0)
ANY = pl.BlockSpec(memory_space=pl.ANY)
PARAMS = pltpu.CompilerParams(vmem_limit_bytes=16 * 1024 * 1024)
LONG = pl.CostEstimate(flops=10**10, bytes_accessed=4 * 1024 * 1024, transcendentals=0)


def place_of(index, count):
    return lax.rem(count - jnp.where(index % 2 == 0, index // 2, count - (index + 1) // 2), count)


def index_at(place, count):
    place = lax.rem(2 * count - place, count)
    return jnp.where(place < count // 2, 2 * place, 2 * (count - place) - 1)


def query_kernel(modules, pairs, x_ref, *refs):
    chunks, rows, sems = refs[:-2], refs[-2], refs[-1]
    queries = chunks[0].shape[1]
    own = pairs // len(chunks)
    span = own * modules
    copies = [
        pltpu.make_async_copy(x_ref.at[:, pl.ds(c * span, span), :], rows.at[c], sems.at[c])
        for c in range(len(chunks))
    ]
    for copy in copies:
        copy.start()
    for c, o_ref in enumerate(chunks):
        copies[c].wait()
        flat = rows.at[c].reshape(queries * span, LANES)
        for m in range(modules):
            for i in range(own):
                got = flat[pl.ds(i * modules + m, queries, stride=span), :]
                o_ref[m * own + i] = got.astype(jnp.bfloat16)


def token_kernel(modules, rank, x_ref, w_ref, a_ref, b_ref, n_ref, rows, wide, sem):
    tokens = x_ref.shape[0] // modules
    copy = pltpu.make_async_copy(x_ref, rows, sem)
    copy.start()
    copy.wait()
    wide[...] = rows[...].astype(jnp.float32)
    norm = jnp.zeros((1, tokens), jnp.float32)
    for m in range(modules):
        turned = wide[pl.ds(m, tokens, stride=modules), :].T
        act, grad = turned[:rank], turned[rank:]
        norm += jnp.sum(act * act, axis=0, keepdims=True) * jnp.sum(
            grad * grad, axis=0, keepdims=True
        )
        grad = grad.astype(jnp.bfloat16)
        w_ref[m, :rank] = grad
        w_ref[m, rank : 2 * rank] = jnp.zeros_like(grad)
        w_ref[m, 2 * rank :] = grad
        a_ref[m] = act
        b_ref[m] = act.astype(jnp.bfloat16)
    n_ref[...] = jnp.broadcast_to(norm, n_ref.shape)


def lane_squares(chunks):
    total = jnp.zeros((GROUP, LANES), jnp.float32)
    for chunk in chunks:
        for k in range(chunk.shape[0]):
            v = chunk[k].astype(jnp.float32)
            total += v * v
    return total


def last_kernel(part, parts, modules, rank, chunk, w_ref, a_ref, *refs):
    before, o_ref = refs[:-1], refs[-1]
    tokens = w_ref.shape[2]
    own = rank // 2 // parts
    step = min(8, own)
    squares = lane_squares([chunk])
    o_ref[:, tokens:] = before[0][:, tokens:] + squares if before else squares
    for lanes in tiles(tokens):
        acc = before[0][:, lanes] if before else jnp.zeros((GROUP, lanes.stop - lanes.start), jnp.float32)
        for m in range(modules):
            for odd in range(2):
                w = w_ref[m, odd * rank : (odd + 2) * rank, lanes]
                for i in range(0, own, step):
                    k = m * own + i
                    left = chunk[k : k + step].reshape(step * GROUP, LANES)
                    inner = jnp.dot(left, w, preferred_element_type=jnp.float32)
                    for s in range(step):
                        row = 2 * (part * own + i + s) + odd
                        acc += inner[s * GROUP : (s + 1) * GROUP] * a_ref[m, row : row + 1, lanes]
        o_ref[:, lanes] = acc


def products(blocks, part, parts, modules, rank, w_ref, b_ref, lanes):
    own = rank // 2 // parts
    step = min(4, own)
    acc = jnp.zeros((len(blocks) * GROUP, lanes.stop - lanes.start), jnp.float32)
    for m in range(modules):
        grad = w_ref[m, :rank, lanes]
        for i in range(0, own, step):
            k = m * own + i
            row = 2 * (part * own + i)
            left = jnp.concatenate(
                [jnp.concatenate([block[k + s] for block in blocks], axis=0) for s in range(step)],
                axis=1,
            )
            right = jnp.concatenate(
                [grad * b_ref[m, row + s : row + s + 1, lanes] for s in range(2 * step)], axis=0
            )
            acc += jnp.dot(left, right, preferred_element_type=jnp.float32)
    return acc


def tiles(tokens):
    size = 512 if tokens % 512 == 0 else tokens
    return [slice(t, t + size) for t in range(0, tokens, size)]


def early_kernel(count, parts, modules, rank, *refs):
    blocks = refs[:count]
    w_ref, b_ref, o_ref = refs[count:]
    tokens = w_ref.shape[2]
    for b in range(count):
        o_ref[b * GROUP : (b + 1) * GROUP, tokens:] = lane_squares(blocks[b : b + 1])

    for lanes in tiles(tokens):
        o_ref[:, lanes] = products(blocks, parts - 1, parts, modules, rank, w_ref, b_ref, lanes)


def late_kernel(count, parts, modules, rank, ring, *refs):
    blocks = refs[:count]
    w_ref, b_ref, n_ref, sum_ref, keep_ref, send_ref, both = refs[count:]
    tokens = w_ref.shape[2]
    half = keep_ref.shape[0] // GROUP
    send_ref[half * GROUP :, :tokens] = n_ref[...]
    for b in range(count):
        span = slice(b * GROUP, (b + 1) * GROUP)
        both[span, tokens:] = sum_ref[span, tokens:] + lane_squares(blocks[b : b + 1])

    for lanes in tiles(tokens):
        both[:, lanes] = sum_ref[:, lanes] + products(
            blocks, 0, parts, modules, rank, w_ref, b_ref, lanes
        )

    me = lax.axis_index("proj")
    for b, index in enumerate(ring()):
        rows = both[b * GROUP : (b + 1) * GROUP]
        at = pl.multiple_of(lax.rem(index, half) * GROUP, GROUP)

        @pl.when(index // half == me)
        def _():
            keep_ref[pl.ds(at, GROUP), :] = rows

        @pl.when(index // half != me)
        def _():
            send_ref[pl.ds(at, GROUP), :] = rows


def scaled(rows, tokens, width, token_scale):
    square = jnp.sum(rows[:, tokens:], axis=1, keepdims=True)
    return rows[:, :tokens] * lax.rsqrt(square / width + epsilon) * token_scale


def most_kernel(width, keep_ref, far_ref, n_ref, o_ref, s_ref):
    rows, tokens = o_ref.shape
    norm = n_ref[...] + far_ref[rows:, :tokens]
    scale = lax.rsqrt(norm / width + epsilon) / jnp.sqrt(jnp.float32(width))
    s_ref[...] = scale
    o_ref[...] = scaled(keep_ref[...] + far_ref[:rows], tokens, width, scale[:1])


def rest_kernel(width, ring, own_ref, far_ref, s_ref, most_ref, o_ref, rows, sem):
    del most_ref
    tokens = o_ref.shape[1]
    half = o_ref.shape[0] // GROUP
    index = ring()

    @pl.when(index // half == lax.axis_index("proj"))
    def _():
        rows[...] = scaled(own_ref[...] + far_ref[...], tokens, width, s_ref[:1])
        at = pl.multiple_of(lax.rem(index, half) * GROUP, GROUP)
        copy = pltpu.make_async_copy(rows, o_ref.at[pl.ds(at, GROUP), :], sem)
        copy.start()
        copy.wait()


def local(train_factors, query_grads):
    tokens, modules, doubled = train_factors.shape
    rank = doubled // 2
    pairs = rank // 2
    ex, proj = lax.axis_size("ex"), lax.axis_size("proj")
    queries = query_grads.shape[0]
    width = modules * proj * rank * rank
    wide = tokens + LANES
    columns = queries * ex // proj

    token_rows = train_factors.reshape(tokens * modules, doubled)
    weights, acts, narrow, norm = pl.pallas_call(
        functools.partial(token_kernel, modules, rank),
        out_shape=(
            jax.ShapeDtypeStruct((modules, 3 * rank, tokens), jnp.bfloat16),
            jax.ShapeDtypeStruct((modules, rank, tokens), jnp.float32),
            jax.ShapeDtypeStruct((modules, rank, tokens), jnp.bfloat16),
            jax.ShapeDtypeStruct((8, tokens), jnp.float32),
        ),
        in_specs=[HBM],
        out_specs=(VMEM,) * 4,
        scratch_shapes=[
            pltpu.VMEM((tokens * modules, doubled), jnp.bfloat16),
            pltpu.VMEM((tokens * modules, doubled), jnp.float32),
            pltpu.SemaphoreType.DMA,
        ],
        compiler_params=PARAMS,
        name="tokens",
    )(pltpu.with_memory_space_constraint(token_rows, pltpu.HBM))

    def swapped(x):
        return lax.ppermute(x, "proj", [(i, (i + 1) % proj) for i in range(proj)])

    def bulk(blocks, ring):
        count, parts = len(blocks), len(blocks[0])
        early = pl.pallas_call(
            functools.partial(early_kernel, count, parts, modules, rank),
            out_shape=jax.ShapeDtypeStruct((count * GROUP, wide), jnp.float32),
            in_specs=[VMEM] * (count + 2),
            out_specs=VMEM,
            compiler_params=PARAMS,
            cost_estimate=COVER,
            name="early",
        )(*[block[-1] for block in blocks], weights, narrow)
        return pl.pallas_call(
            functools.partial(late_kernel, count, parts, modules, rank, ring),
            out_shape=(
                jax.ShapeDtypeStruct((columns, wide), jnp.float32),
                jax.ShapeDtypeStruct((columns + 8, wide), jnp.float32),
            ),
            in_specs=[VMEM] * (count + 4),
            out_specs=(VMEM, VMEM),
            scratch_shapes=[pltpu.VMEM((count * GROUP, wide), jnp.float32)],
            compiler_params=PARAMS,
            cost_estimate=COVER,
            name="late",
        )(*[block[0] for block in blocks], weights, narrow, norm, early)

    def most(keep, far):
        return pl.pallas_call(
            functools.partial(most_kernel, width),
            out_shape=(
                jax.ShapeDtypeStruct((columns, tokens), jnp.float32),
                jax.ShapeDtypeStruct((8, tokens), jnp.float32),
            ),
            in_specs=[VMEM] * 3,
            out_specs=(VMEM, VMEM),
            compiler_params=PARAMS,
            cost_estimate=LONG,
            name="most",
        )(keep, far, norm)

    if queries == GROUP and ex % 2 == 0 and ex <= 16:
        order = list(range(0, ex, 2)) + list(range(ex - 1, 0, -2))
        order = order[:1] + order[:0:-1]
        up_pairs = [(order[i], order[(i + 1) % ex]) for i in range(ex)]
        down_pairs = [(b, a) for a, b in up_pairs]

        def up(x):
            return lax.ppermute(x, "ex", up_pairs)

        def down(x):
            return lax.ppermute(x, "ex", down_pairs)

        rows = query_grads.reshape(queries, modules, pairs, LANES)
        rows = rows.transpose(0, 2, 1, 3).reshape(queries, pairs * modules, LANES)
        chunk = jax.ShapeDtypeStruct((modules * pairs // 2, queries, LANES), jnp.bfloat16)
        block = pl.pallas_call(
            functools.partial(query_kernel, modules, pairs),
            out_shape=(chunk, chunk),
            in_specs=[HBM],
            out_specs=(VMEM, VMEM),
            scratch_shapes=[
                pltpu.VMEM((2, queries, pairs * modules // 2, LANES), jnp.float32),
                pltpu.SemaphoreType.DMA((2,)),
            ],
            compiler_params=PARAMS,
            name="queries",
        )(pltpu.with_memory_space_constraint(rows, pltpu.HBM))
        below, above = block, block
        blocks, steps = [block], [0]
        for step in range(1, ex // 2):
            first = (up(below[0]), down(above[0]))
            second = (up(below[1]), down(above[1]))
            if step == 1:
                arrived, weights = lax.optimization_barrier((first[0], weights))
                first = (arrived, first[1])
            below, above = (first[0], second[0]), (first[1], second[1])
            blocks += [below, above]
            steps += [-step, step]
        across = (up(below[0]), down(above[1]))

        def ring():
            here = place_of(lax.axis_index("ex"), ex)
            return [index_at(here + step, ex) for step in steps]

        def opposite():
            return index_at(place_of(lax.axis_index("ex"), ex) + ex // 2, ex)

        keep, send = bulk(blocks, ring)
        out, scale = most(keep, swapped(send))
        mine = ()
        for part, chunk in enumerate(across):
            mine = (
                pl.pallas_call(
                    functools.partial(last_kernel, part, len(across), modules, rank),
                    out_shape=jax.ShapeDtypeStruct((GROUP, wide), jnp.float32),
                    in_specs=[VMEM] * (3 + len(mine)),
                    out_specs=VMEM,
                    compiler_params=PARAMS,
                    cost_estimate=LONG if part else COVER,
                    name="last",
                )(chunk, weights, acts, *mine),
            )
        (mine,) = mine
        out = pl.pallas_call(
            functools.partial(rest_kernel, width, opposite),
            out_shape=jax.ShapeDtypeStruct((columns, tokens), jnp.float32),
            in_specs=[VMEM, VMEM, VMEM, ANY],
            out_specs=ANY,
            scratch_shapes=[pltpu.VMEM((GROUP, tokens), jnp.float32), pltpu.SemaphoreType.DMA],
            input_output_aliases={3: 0},
            compiler_params=PARAMS,
            name="rest",
        )(mine, swapped(mine), scale, out)
    else:
        gathered = lax.all_gather(query_grads.astype(jnp.bfloat16), "ex", axis=0, tiled=True)
        count = queries * ex // GROUP
        gathered = gathered.reshape(count, GROUP, modules, 2, pairs // 2, LANES)
        gathered = gathered.transpose(0, 3, 2, 4, 1, 5).reshape(count, 2, -1, GROUP, LANES)
        blocks = [(gathered[i, 0], gathered[i, 1]) for i in range(count)]
        keep, send = bulk(blocks, lambda: [jnp.int32(i) for i in range(count)])
        out, _ = most(keep, swapped(send))
    return out.T


def solution(mesh):
    return jax.shard_map(
        local,
        mesh=mesh,
        in_specs=(P(("groups", "ex"), "proj", None), P(("groups", "ex"), "proj", None)),
        out_specs=P(("groups", "ex"), "proj"),
        check_vma=False,
    )
```

```python
import functools

import jax
import jax.numpy as jnp
from jax import lax
from jax.experimental import pallas as pl
from jax.experimental.pallas import tpu as pltpu
from jax.sharding import PartitionSpec as P

epsilon = 1e-06
LANES = 128
GROUP = 16
VMEM = pl.BlockSpec(memory_space=pltpu.VMEM)
HBM = pl.BlockSpec(memory_space=pltpu.HBM)
COVER = pl.CostEstimate(flops=692100000, bytes_accessed=1024, transcendentals=0)
ANY = pl.BlockSpec(memory_space=pl.ANY)
PARAMS = pltpu.CompilerParams(vmem_limit_bytes=16 * 1024 * 1024)
LONG = pl.CostEstimate(flops=10**10, bytes_accessed=4 * 1024 * 1024, transcendentals=0)


def place_of(index, count):
    return lax.rem(count - jnp.where(index % 2 == 0, index // 2, count - (index + 1) // 2), count)


def index_at(place, count):
    place = lax.rem(2 * count - place, count)
    return jnp.where(place < count // 2, 2 * place, 2 * (count - place) - 1)


def query_kernel(modules, pairs, x_ref, *refs):
    chunks, rows, sems = refs[:-2], refs[-2], refs[-1]
    queries = chunks[0].shape[1]
    own = pairs // len(chunks)
    span = own * modules
    copies = [
        pltpu.make_async_copy(x_ref.at[:, pl.ds(c * span, span), :], rows.at[c], sems.at[c])
        for c in range(len(chunks))
    ]
    for copy in copies:
        copy.start()
    for c, o_ref in enumerate(chunks):
        copies[c].wait()
        flat = rows.at[c].reshape(queries * span, LANES)
        for m in range(modules):
            for i in range(own):
                got = flat[pl.ds(i * modules + m, queries, stride=span), :]
                o_ref[m * own + i] = got.astype(jnp.bfloat16)


def token_kernel(modules, rank, x_ref, p_ref, n_ref, rows, wide, sem):
    tokens = x_ref.shape[0] // modules
    copy = pltpu.make_async_copy(x_ref, rows, sem)
    copy.start()
    copy.wait()
    wide[...] = rows[...].astype(jnp.float32)
    norm = jnp.zeros((1, tokens), jnp.float32)
    for m in range(modules):
        turned = wide[pl.ds(m, tokens, stride=modules), :].T
        act, grad = turned[:rank], turned[rank:]
        norm += jnp.sum(act * act, axis=0, keepdims=True) * jnp.sum(
            grad * grad, axis=0, keepdims=True
        )
        p_ref[0, m] = act.astype(jnp.bfloat16)
        p_ref[1, m] = grad.astype(jnp.bfloat16)
    n_ref[...] = jnp.broadcast_to(norm, n_ref.shape)


def lane_squares(chunks):
    total = jnp.zeros((GROUP, LANES), jnp.float32)
    for chunk in chunks:
        for k in range(chunk.shape[0]):
            v = chunk[k].astype(jnp.float32)
            total += v * v
    return total


def last_kernel(part, parts, modules, rank, chunk, p_ref, *refs):
    before, o_ref = refs[:-1], refs[-1]
    tokens = p_ref.shape[3]
    own = rank // 2 // parts
    step = min(8, own)
    squares = lane_squares([chunk])
    o_ref[:, tokens:] = before[0][:, tokens:] + squares if before else squares
    for lanes in tiles(tokens):
        acc = before[0][:, lanes] if before else jnp.zeros((GROUP, lanes.stop - lanes.start), jnp.float32)
        for m in range(modules):
            act = p_ref[0, m, 2 * part * own : 2 * (part + 1) * own, lanes].astype(jnp.float32)
            grad = p_ref[1, m, :, lanes]
            for odd in range(2):
                for i in range(0, own, step):
                    k = m * own + i
                    left = chunk[k : k + step].reshape(step * GROUP, LANES)
                    left = left[:, odd * rank : (odd + 1) * rank]
                    inner = jnp.dot(left, grad, preferred_element_type=jnp.float32)
                    for s in range(step):
                        row = 2 * (i + s) + odd
                        acc += inner[s * GROUP : (s + 1) * GROUP] * act[row : row + 1]
        o_ref[:, lanes] = acc


def products(blocks, part, parts, modules, rank, p_ref, lanes):
    own = rank // 2 // parts
    step = min(4, own)
    acc = jnp.zeros((len(blocks) * GROUP, lanes.stop - lanes.start), jnp.float32)
    for m in range(modules):
        grad = p_ref[1, m, :, lanes]
        for i in range(0, own, step):
            k = m * own + i
            row = 2 * (part * own + i)
            left = jnp.concatenate(
                [jnp.concatenate([block[k + s] for block in blocks], axis=0) for s in range(step)],
                axis=1,
            )
            right = jnp.concatenate(
                [grad * p_ref[0, m, row + s : row + s + 1, lanes] for s in range(2 * step)], axis=0
            )
            acc += jnp.dot(left, right, preferred_element_type=jnp.float32)
    return acc


def tiles(tokens):
    size = 512 if tokens % 512 == 0 else tokens
    return [slice(t, t + size) for t in range(0, tokens, size)]


def early_kernel(count, parts, modules, rank, *refs):
    blocks = refs[:count]
    p_ref, o_ref = refs[count:]
    tokens = p_ref.shape[3]
    for b in range(count):
        o_ref[b * GROUP : (b + 1) * GROUP, tokens:] = lane_squares(blocks[b : b + 1])

    for lanes in tiles(tokens):
        o_ref[:, lanes] = products(blocks, parts - 1, parts, modules, rank, p_ref, lanes)


def late_kernel(count, parts, modules, rank, ring, *refs):
    blocks = refs[:count]
    p_ref, n_ref, sum_ref, keep_ref, send_ref, both = refs[count:]
    tokens = p_ref.shape[3]
    half = keep_ref.shape[0] // GROUP
    send_ref[half * GROUP :, :tokens] = n_ref[...]
    for b in range(count):
        span = slice(b * GROUP, (b + 1) * GROUP)
        both[span, tokens:] = sum_ref[span, tokens:] + lane_squares(blocks[b : b + 1])

    for lanes in tiles(tokens):
        both[:, lanes] = sum_ref[:, lanes] + products(
            blocks, 0, parts, modules, rank, p_ref, lanes
        )

    me = lax.axis_index("proj")
    for b, index in enumerate(ring()):
        rows = both[b * GROUP : (b + 1) * GROUP]
        at = pl.multiple_of(lax.rem(index, half) * GROUP, GROUP)

        @pl.when(index // half == me)
        def _():
            keep_ref[pl.ds(at, GROUP), :] = rows

        @pl.when(index // half != me)
        def _():
            send_ref[pl.ds(at, GROUP), :] = rows


def scaled(rows, tokens, width, token_scale):
    square = jnp.sum(rows[:, tokens:], axis=1, keepdims=True)
    return rows[:, :tokens] * lax.rsqrt(square / width + epsilon) * token_scale


def most_kernel(width, keep_ref, far_ref, n_ref, o_ref, s_ref):
    rows, tokens = o_ref.shape
    norm = n_ref[...] + far_ref[rows:, :tokens]
    scale = lax.rsqrt(norm / width + epsilon) / jnp.sqrt(jnp.float32(width))
    s_ref[...] = scale
    o_ref[...] = scaled(keep_ref[...] + far_ref[:rows], tokens, width, scale[:1])


def rest_kernel(width, ring, own_ref, far_ref, s_ref, most_ref, o_ref, rows, sem):
    del most_ref
    tokens = o_ref.shape[1]
    half = o_ref.shape[0] // GROUP
    index = ring()

    @pl.when(index // half == lax.axis_index("proj"))
    def _():
        rows[...] = scaled(own_ref[...] + far_ref[...], tokens, width, s_ref[:1])
        at = pl.multiple_of(lax.rem(index, half) * GROUP, GROUP)
        copy = pltpu.make_async_copy(rows, o_ref.at[pl.ds(at, GROUP), :], sem)
        copy.start()
        copy.wait()


def local(train_factors, query_grads):
    tokens, modules, doubled = train_factors.shape
    rank = doubled // 2
    pairs = rank // 2
    ex, proj = lax.axis_size("ex"), lax.axis_size("proj")
    queries = query_grads.shape[0]
    width = modules * proj * rank * rank
    wide = tokens + LANES
    columns = queries * ex // proj

    token_rows = train_factors.reshape(tokens * modules, doubled)
    factors, norm = pl.pallas_call(
        functools.partial(token_kernel, modules, rank),
        out_shape=(
            jax.ShapeDtypeStruct((2, modules, rank, tokens), jnp.bfloat16),
            jax.ShapeDtypeStruct((8, tokens), jnp.float32),
        ),
        in_specs=[HBM],
        out_specs=(VMEM, VMEM),
        scratch_shapes=[
            pltpu.VMEM((tokens * modules, doubled), jnp.bfloat16),
            pltpu.VMEM((tokens * modules, doubled), jnp.float32),
            pltpu.SemaphoreType.DMA,
        ],
        compiler_params=PARAMS,
        name="tokens",
    )(pltpu.with_memory_space_constraint(token_rows, pltpu.HBM))

    def swapped(x):
        return lax.ppermute(x, "proj", [(i, (i + 1) % proj) for i in range(proj)])

    def bulk(blocks, ring):
        count, parts = len(blocks), len(blocks[0])
        early = pl.pallas_call(
            functools.partial(early_kernel, count, parts, modules, rank),
            out_shape=jax.ShapeDtypeStruct((count * GROUP, wide), jnp.float32),
            in_specs=[VMEM] * (count + 1),
            out_specs=VMEM,
            compiler_params=PARAMS,
            cost_estimate=COVER,
            name="early",
        )(*[block[-1] for block in blocks], factors)
        return pl.pallas_call(
            functools.partial(late_kernel, count, parts, modules, rank, ring),
            out_shape=(
                jax.ShapeDtypeStruct((columns, wide), jnp.float32),
                jax.ShapeDtypeStruct((columns + 8, wide), jnp.float32),
            ),
            in_specs=[VMEM] * (count + 3),
            out_specs=(VMEM, VMEM),
            scratch_shapes=[pltpu.VMEM((count * GROUP, wide), jnp.float32)],
            compiler_params=PARAMS,
            cost_estimate=COVER,
            name="late",
        )(*[block[0] for block in blocks], factors, norm, early)

    def most(keep, far):
        return pl.pallas_call(
            functools.partial(most_kernel, width),
            out_shape=(
                jax.ShapeDtypeStruct((columns, tokens), jnp.float32),
                jax.ShapeDtypeStruct((8, tokens), jnp.float32),
            ),
            in_specs=[VMEM] * 3,
            out_specs=(VMEM, VMEM),
            compiler_params=PARAMS,
            cost_estimate=LONG,
            name="most",
        )(keep, far, norm)

    if queries == GROUP and ex % 2 == 0 and ex <= 16:
        order = list(range(0, ex, 2)) + list(range(ex - 1, 0, -2))
        order = order[:1] + order[:0:-1]
        up_pairs = [(order[i], order[(i + 1) % ex]) for i in range(ex)]
        down_pairs = [(b, a) for a, b in up_pairs]

        def up(x):
            return lax.ppermute(x, "ex", up_pairs)

        def down(x):
            return lax.ppermute(x, "ex", down_pairs)

        rows = query_grads.reshape(queries, modules, pairs, LANES)
        rows = rows.transpose(0, 2, 1, 3).reshape(queries, pairs * modules, LANES)
        chunk = jax.ShapeDtypeStruct((modules * pairs // 2, queries, LANES), jnp.bfloat16)
        block = pl.pallas_call(
            functools.partial(query_kernel, modules, pairs),
            out_shape=(chunk, chunk),
            in_specs=[HBM],
            out_specs=(VMEM, VMEM),
            scratch_shapes=[
                pltpu.VMEM((2, queries, pairs * modules // 2, LANES), jnp.float32),
                pltpu.SemaphoreType.DMA((2,)),
            ],
            compiler_params=PARAMS,
            name="queries",
        )(pltpu.with_memory_space_constraint(rows, pltpu.HBM))
        below, above = block, block
        blocks, steps = [block], [0]
        for step in range(1, ex // 2):
            first = (up(below[0]), down(above[0]))
            second = (up(below[1]), down(above[1]))
            if step == 1:
                arrived, factors = lax.optimization_barrier((first[0], factors))
                first = (arrived, first[1])
            below, above = (first[0], second[0]), (first[1], second[1])
            blocks += [below, above]
            steps += [-step, step]
        across = (up(below[0]), down(above[1]))

        def ring():
            here = place_of(lax.axis_index("ex"), ex)
            return [index_at(here + step, ex) for step in steps]

        def opposite():
            return index_at(place_of(lax.axis_index("ex"), ex) + ex // 2, ex)

        keep, send = bulk(blocks, ring)
        out, scale = most(keep, swapped(send))
        mine = ()
        for part, chunk in enumerate(across):
            mine = (
                pl.pallas_call(
                    functools.partial(last_kernel, part, len(across), modules, rank),
                    out_shape=jax.ShapeDtypeStruct((GROUP, wide), jnp.float32),
                    in_specs=[VMEM] * (2 + len(mine)),
                    out_specs=VMEM,
                    compiler_params=PARAMS,
                    cost_estimate=LONG if part else COVER,
                    name="last",
                )(chunk, factors, *mine),
            )
        (mine,) = mine
        out = pl.pallas_call(
            functools.partial(rest_kernel, width, opposite),
            out_shape=jax.ShapeDtypeStruct((columns, tokens), jnp.float32),
            in_specs=[VMEM, VMEM, VMEM, ANY],
            out_specs=ANY,
            scratch_shapes=[pltpu.VMEM((GROUP, tokens), jnp.float32), pltpu.SemaphoreType.DMA],
            input_output_aliases={3: 0},
            compiler_params=PARAMS,
            name="rest",
        )(mine, swapped(mine), scale, out)
    else:
        gathered = lax.all_gather(query_grads.astype(jnp.bfloat16), "ex", axis=0, tiled=True)
        count = queries * ex // GROUP
        gathered = gathered.reshape(count, GROUP, modules, 2, pairs // 2, LANES)
        gathered = gathered.transpose(0, 3, 2, 4, 1, 5).reshape(count, 2, -1, GROUP, LANES)
        blocks = [(gathered[i, 0], gathered[i, 1]) for i in range(count)]
        keep, send = bulk(blocks, lambda: [jnp.int32(i) for i in range(count)])
        out, _ = most(keep, swapped(send))
    return out.T


def solution(mesh):
    return jax.shard_map(
        local,
        mesh=mesh,
        in_specs=(P(("groups", "ex"), "proj", None), P(("groups", "ex"), "proj", None)),
        out_specs=P(("groups", "ex"), "proj"),
        check_vma=False,
    )
```

```python
import functools

import jax
import jax.numpy as jnp
from jax import lax
from jax.experimental import pallas as pl
from jax.experimental.pallas import tpu as pltpu
from jax.sharding import PartitionSpec as P

epsilon = 1e-06
LANES = 128
GROUP = 16
VMEM = pl.BlockSpec(memory_space=pltpu.VMEM)
HBM = pl.BlockSpec(memory_space=pltpu.HBM)


def cover(share):
    return pl.CostEstimate(flops=int(share * 10**9), bytes_accessed=1024, transcendentals=0)


ANY = pl.BlockSpec(memory_space=pl.ANY)
PARAMS = pltpu.CompilerParams(vmem_limit_bytes=16 * 1024 * 1024)
LONG = pl.CostEstimate(flops=10**10, bytes_accessed=4 * 1024 * 1024, transcendentals=0)


def place_of(index, count):
    return lax.rem(count - jnp.where(index % 2 == 0, index // 2, count - (index + 1) // 2), count)


def index_at(place, count):
    place = lax.rem(2 * count - place, count)
    return jnp.where(place < count // 2, 2 * place, 2 * (count - place) - 1)


def query_kernel(modules, pairs, x_ref, *refs):
    chunks, rows, sems = refs[:-2], refs[-2], refs[-1]
    queries = chunks[0].shape[1]
    own = pairs // len(chunks)
    span = own * modules
    copies = [
        pltpu.make_async_copy(x_ref.at[:, pl.ds(c * span, span), :], rows.at[c], sems.at[c])
        for c in range(len(chunks))
    ]
    for copy in copies:
        copy.start()
    for c, o_ref in enumerate(chunks):
        copies[c].wait()
        flat = rows.at[c].reshape(queries * span, LANES)
        for m in range(modules):
            for i in range(own):
                got = flat[pl.ds(i * modules + m, queries, stride=span), :]
                o_ref[m * own + i] = got.astype(jnp.bfloat16)


def token_kernel(modules, rank, core, x_ref, *refs):
    p_ref, n_ref, rows, wide, sem = refs[-5:]
    tokens = x_ref.shape[0] // modules

    def run():
        copy = pltpu.make_async_copy(x_ref, rows, sem)
        copy.start()
        copy.wait()
        wide[...] = rows[...].astype(jnp.float32)
        norm = jnp.zeros((1, tokens), jnp.float32)
        for m in range(modules):
            turned = wide[pl.ds(m, tokens, stride=modules), :].T
            act, grad = turned[:rank], turned[rank:]
            norm += jnp.sum(act * act, axis=0, keepdims=True) * jnp.sum(
                grad * grad, axis=0, keepdims=True
            )
            p_ref[0, m] = act.astype(jnp.bfloat16)
            p_ref[1, m] = grad.astype(jnp.bfloat16)
        n_ref[...] = jnp.broadcast_to(norm, n_ref.shape)

    if core is None:
        run()
    else:
        pl.when((lax.axis_index("proj") == 0) == (core == 0))(run)


def lane_squares(chunks):
    total = jnp.zeros((GROUP, LANES), jnp.float32)
    for chunk in chunks:
        for k in range(chunk.shape[0]):
            v = chunk[k].astype(jnp.float32)
            total += v * v
    return total


def last_kernel(part, parts, modules, rank, chunk, p_ref, *refs):
    before, o_ref = refs[:-1], refs[-1]
    tokens = p_ref.shape[3]
    own = rank // 2 // parts
    step = min(8, own)
    squares = lane_squares([chunk])
    o_ref[:, tokens:] = before[0][:, tokens:] + squares if before else squares
    for lanes in tiles(tokens):
        acc = before[0][:, lanes] if before else jnp.zeros((GROUP, lanes.stop - lanes.start), jnp.float32)
        for m in range(modules):
            act = p_ref[0, m, 2 * part * own : 2 * (part + 1) * own, lanes].astype(jnp.float32)
            grad = p_ref[1, m, :, lanes]
            for odd in range(2):
                for i in range(0, own, step):
                    k = m * own + i
                    left = chunk[k : k + step].reshape(step * GROUP, LANES)
                    left = left[:, odd * rank : (odd + 1) * rank]
                    inner = jnp.dot(left, grad, preferred_element_type=jnp.float32)
                    for s in range(step):
                        row = 2 * (i + s) + odd
                        acc += inner[s * GROUP : (s + 1) * GROUP] * act[row : row + 1]
        o_ref[:, lanes] = acc


def products(blocks, part, parts, modules, rank, p_ref, lanes):
    own = rank // 2 // parts
    step = min(4, own)
    acc = jnp.zeros((len(blocks) * GROUP, lanes.stop - lanes.start), jnp.float32)
    for m in range(modules):
        grad = p_ref[1, m, :, lanes]
        for i in range(0, own, step):
            k = m * own + i
            row = 2 * (part * own + i)
            left = jnp.concatenate(
                [jnp.concatenate([block[k + s] for block in blocks], axis=0) for s in range(step)],
                axis=1,
            )
            right = jnp.concatenate(
                [grad * p_ref[0, m, row + s : row + s + 1, lanes] for s in range(2 * step)], axis=0
            )
            acc += jnp.dot(left, right, preferred_element_type=jnp.float32)
    return acc


def tiles(tokens):
    size = 512 if tokens % 512 == 0 else tokens
    return [slice(t, t + size) for t in range(0, tokens, size)]


def early_kernel(count, parts, modules, rank, *refs):
    blocks = refs[:count]
    p_ref, o_ref = refs[count:]
    tokens = p_ref.shape[3]
    for b in range(count):
        o_ref[b * GROUP : (b + 1) * GROUP, tokens:] = lane_squares(blocks[b : b + 1])
    for lanes in tiles(tokens):
        o_ref[:, lanes] = products(blocks, 0, parts, modules, rank, p_ref, lanes)


def late_kernel(count, parts, modules, rank, *refs):
    blocks = refs[:count]
    p_ref, sum_ref, o_ref = refs[count:]
    tokens = p_ref.shape[3]
    known = sum_ref.shape[0]
    for b in range(count):
        o_ref[b * GROUP : (b + 1) * GROUP, tokens:] = lane_squares(blocks[b : b + 1])
    for lanes in tiles(tokens):
        o_ref[:, lanes] = products(blocks, parts - 1, parts, modules, rank, p_ref, lanes)
    o_ref[:known] += sum_ref[...]


def third_kernel(count, parts, modules, rank, ring, chunk, p_ref, n_ref, sum_ref, keep_ref, send_ref, last):
    tokens = p_ref.shape[3]
    half = keep_ref.shape[0] // GROUP
    first = (count - 1) * GROUP
    last_kernel(0, parts, modules, rank, chunk, p_ref, sum_ref.at[first:], last)
    send_ref[half * GROUP :, :tokens] = n_ref[...]
    me = lax.axis_index("proj")
    for b, index in enumerate(ring()):
        rows = last[...] if b == count - 1 else sum_ref[b * GROUP : (b + 1) * GROUP]
        at = pl.multiple_of(lax.rem(index, half) * GROUP, GROUP)

        @pl.when(index // half == me)
        def _():
            keep_ref[pl.ds(at, GROUP), :] = rows

        @pl.when(index // half != me)
        def _():
            send_ref[pl.ds(at, GROUP), :] = rows


def scaled(rows, tokens, width, token_scale):
    square = jnp.sum(rows[:, tokens:], axis=1, keepdims=True)
    return rows[:, :tokens] * lax.rsqrt(square / width + epsilon) * token_scale


def most_kernel(width, keep_ref, far_ref, n_ref, o_ref, s_ref):
    rows, tokens = o_ref.shape
    norm = n_ref[...] + far_ref[rows:, :tokens]
    scale = lax.rsqrt(norm / width + epsilon) / jnp.sqrt(jnp.float32(width))
    s_ref[...] = scale
    o_ref[...] = scaled(keep_ref[...] + far_ref[:rows], tokens, width, scale[:1])


def rest_kernel(width, ring, own_ref, far_ref, s_ref, most_ref, o_ref, rows, sem):
    del most_ref
    tokens = o_ref.shape[1]
    half = o_ref.shape[0] // GROUP
    index = ring()

    @pl.when(index // half == lax.axis_index("proj"))
    def _():
        rows[...] = scaled(own_ref[...] + far_ref[...], tokens, width, s_ref[:1])
        at = pl.multiple_of(lax.rem(index, half) * GROUP, GROUP)
        copy = pltpu.make_async_copy(rows, o_ref.at[pl.ds(at, GROUP), :], sem)
        copy.start()
        copy.wait()


def local(train_factors, query_grads):
    tokens, modules, doubled = train_factors.shape
    rank = doubled // 2
    pairs = rank // 2
    ex, proj = lax.axis_size("ex"), lax.axis_size("proj")
    queries = query_grads.shape[0]
    width = modules * proj * rank * rank
    wide = tokens + LANES
    columns = queries * ex // proj

    token_rows = train_factors.reshape(tokens * modules, doubled)
    def token_work(core, *before):
        return pl.pallas_call(
            functools.partial(token_kernel, modules, rank, core),
            out_shape=(
                jax.ShapeDtypeStruct((2, modules, rank, tokens), jnp.bfloat16),
                jax.ShapeDtypeStruct((8, tokens), jnp.float32),
            ),
            in_specs=[HBM] + [VMEM] * len(before),
            out_specs=(VMEM, VMEM),
            scratch_shapes=[
                pltpu.VMEM((tokens * modules, doubled), jnp.bfloat16),
                pltpu.VMEM((tokens * modules, doubled), jnp.float32),
                pltpu.SemaphoreType.DMA,
            ],
            input_output_aliases={1 + i: i for i in range(len(before))},
            compiler_params=PARAMS,
            name="tokens",
        )(pltpu.with_memory_space_constraint(token_rows, pltpu.HBM), *before)

    def swapped(x):
        return lax.ppermute(x, "proj", [(i, (i + 1) % proj) for i in range(proj)])

    def bulk(blocks, ring, factors, norm):
        count, parts = len(blocks), len(blocks[0])
        early = pl.pallas_call(
            functools.partial(early_kernel, count - 1, parts, modules, rank),
            out_shape=jax.ShapeDtypeStruct(((count - 1) * GROUP, wide), jnp.float32),
            in_specs=[VMEM] * count,
            out_specs=VMEM,
            compiler_params=PARAMS,
            cost_estimate=cover(0.81),
            name="early",
        )(*[block[0] for block in blocks[:-1]], factors)
        late = pl.pallas_call(
            functools.partial(late_kernel, count, parts, modules, rank),
            out_shape=jax.ShapeDtypeStruct((count * GROUP, wide), jnp.float32),
            in_specs=[VMEM] * (count + 2),
            out_specs=VMEM,
            compiler_params=PARAMS,
            cost_estimate=cover(0.58),
            name="late",
        )(*[block[-1] for block in blocks], factors, early)
        return pl.pallas_call(
            functools.partial(third_kernel, count, parts, modules, rank, ring),
            out_shape=(
                jax.ShapeDtypeStruct((columns, wide), jnp.float32),
                jax.ShapeDtypeStruct((columns + 8, wide), jnp.float32),
            ),
            in_specs=[VMEM] * 4,
            out_specs=(VMEM, VMEM),
            scratch_shapes=[pltpu.VMEM((GROUP, wide), jnp.float32)],
            compiler_params=PARAMS,
            cost_estimate=cover(0.23),
            name="third",
        )(blocks[-1][0], factors, norm, late)

    def most(keep, far, norm):
        return pl.pallas_call(
            functools.partial(most_kernel, width),
            out_shape=(
                jax.ShapeDtypeStruct((columns, tokens), jnp.float32),
                jax.ShapeDtypeStruct((8, tokens), jnp.float32),
            ),
            in_specs=[VMEM] * 3,
            out_specs=(VMEM, VMEM),
            compiler_params=PARAMS,
            cost_estimate=LONG,
            name="most",
        )(keep, far, norm)

    if queries == GROUP and ex % 2 == 0 and ex <= 16:
        order = list(range(0, ex, 2)) + list(range(ex - 1, 0, -2))
        order = order[:1] + order[:0:-1]
        up_pairs = [(order[i], order[(i + 1) % ex]) for i in range(ex)]
        down_pairs = [(b, a) for a, b in up_pairs]

        def up(x):
            return lax.ppermute(x, "ex", up_pairs)

        def down(x):
            return lax.ppermute(x, "ex", down_pairs)

        rows = query_grads.reshape(queries, modules, pairs, LANES)
        rows = rows.transpose(0, 2, 1, 3).reshape(queries, pairs * modules, LANES)
        chunk = jax.ShapeDtypeStruct((modules * pairs // 2, queries, LANES), jnp.bfloat16)
        block = pl.pallas_call(
            functools.partial(query_kernel, modules, pairs),
            out_shape=(chunk, chunk),
            in_specs=[HBM],
            out_specs=(VMEM, VMEM),
            scratch_shapes=[
                pltpu.VMEM((2, queries, pairs * modules // 2, LANES), jnp.float32),
                pltpu.SemaphoreType.DMA((2,)),
            ],
            compiler_params=PARAMS,
            name="queries",
        )(pltpu.with_memory_space_constraint(rows, pltpu.HBM))
        factors, norm = token_work(1)
        later = lax.optimization_barrier((block[1], block[0], factors))
        below, above, factors = (block[0], later[0]), (later[1], block[1]), later[2]
        factors, norm = token_work(0, factors, norm)
        blocks, steps = [block], [0]
        for step in range(1, ex // 2):
            first = (up(below[0]), down(above[0]))
            second = (up(below[1]), down(above[1]))
            if step == 1:
                arrived, factors = lax.optimization_barrier((first[0], factors))
                first = (arrived, first[1])
            below, above = (first[0], second[0]), (first[1], second[1])
            blocks += [below, above]
            steps += [-step, step]
        across = (up(below[0]), down(above[1]))

        def ring():
            here = place_of(lax.axis_index("ex"), ex)
            return [index_at(here + step, ex) for step in steps]

        def opposite():
            return index_at(place_of(lax.axis_index("ex"), ex) + ex // 2, ex)

        keep, send = bulk(blocks, ring, factors, norm)
        out, scale = most(keep, swapped(send), norm)
        mine = ()
        for part, chunk in enumerate(across):
            mine = (
                pl.pallas_call(
                    functools.partial(last_kernel, part, len(across), modules, rank),
                    out_shape=jax.ShapeDtypeStruct((GROUP, wide), jnp.float32),
                    in_specs=[VMEM] * (2 + len(mine)),
                    out_specs=VMEM,
                    compiler_params=PARAMS,
                    cost_estimate=LONG if part else cover(0.46),
                    name="last",
                )(chunk, factors, *mine),
            )
        (mine,) = mine
        out = pl.pallas_call(
            functools.partial(rest_kernel, width, opposite),
            out_shape=jax.ShapeDtypeStruct((columns, tokens), jnp.float32),
            in_specs=[VMEM, VMEM, VMEM, ANY],
            out_specs=ANY,
            scratch_shapes=[pltpu.VMEM((GROUP, tokens), jnp.float32), pltpu.SemaphoreType.DMA],
            input_output_aliases={3: 0},
            compiler_params=PARAMS,
            name="rest",
        )(mine, swapped(mine), scale, out)
    else:
        gathered = lax.all_gather(query_grads.astype(jnp.bfloat16), "ex", axis=0, tiled=True)
        count = queries * ex // GROUP
        gathered = gathered.reshape(count, GROUP, modules, 2, pairs // 2, LANES)
        gathered = gathered.transpose(0, 3, 2, 4, 1, 5).reshape(count, 2, -1, GROUP, LANES)
        blocks = [(gathered[i, 0], gathered[i, 1]) for i in range(count)]
        factors, norm = token_work(None)
        keep, send = bulk(blocks, lambda: [jnp.int32(i) for i in range(count)], factors, norm)
        out, _ = most(keep, swapped(send), norm)
    return out.T


def solution(mesh):
    return jax.shard_map(
        local,
        mesh=mesh,
        in_specs=(P(("groups", "ex"), "proj", None), P(("groups", "ex"), "proj", None)),
        out_specs=P(("groups", "ex"), "proj"),
        check_vma=False,
    )
```

```python
import functools

import jax
import jax.numpy as jnp
from jax import lax
from jax.experimental import pallas as pl
from jax.experimental.pallas import tpu as pltpu
from jax.sharding import PartitionSpec as P

epsilon = 1e-06
LANES = 128
GROUP = 16
VMEM = pl.BlockSpec(memory_space=pltpu.VMEM)
HBM = pl.BlockSpec(memory_space=pltpu.HBM)


SHORT = pl.CostEstimate(flops=10**6, bytes_accessed=1024, transcendentals=0)


def cover(share):
    return pl.CostEstimate(flops=int(share * 10**9), bytes_accessed=1024, transcendentals=0)


ANY = pl.BlockSpec(memory_space=pl.ANY)
PARAMS = pltpu.CompilerParams(vmem_limit_bytes=16 * 1024 * 1024)
LONG = pl.CostEstimate(flops=10**10, bytes_accessed=4 * 1024 * 1024, transcendentals=0)


def place_of(index, count):
    return lax.rem(count - jnp.where(index % 2 == 0, index // 2, count - (index + 1) // 2), count)


def index_at(place, count):
    place = lax.rem(2 * count - place, count)
    return jnp.where(place < count // 2, 2 * place, 2 * (count - place) - 1)


def query_kernel(modules, pairs, x_ref, *refs):
    chunks, rows, sems = refs[:-2], refs[-2], refs[-1]
    queries = chunks[0].shape[1]
    own = pairs // len(chunks)
    span = own * modules
    copies = [
        pltpu.make_async_copy(x_ref.at[:, pl.ds(c * span, span), :], rows.at[c], sems.at[c])
        for c in range(len(chunks))
    ]
    for copy in copies:
        copy.start()
    for c, o_ref in enumerate(chunks):
        copies[c].wait()
        flat = rows.at[c].reshape(queries * span, LANES)
        for m in range(modules):
            for i in range(own):
                got = flat[pl.ds(i * modules + m, queries, stride=span), :]
                o_ref[m * own + i] = got.astype(jnp.bfloat16)


def token_kernel(modules, rank, core, x_ref, *refs):
    p_ref, n_ref, rows, wide, sem = refs[-5:]
    tokens = x_ref.shape[0] // modules

    def run():
        copy = pltpu.make_async_copy(x_ref, rows, sem)
        copy.start()
        copy.wait()
        wide[...] = rows[...].astype(jnp.float32)
        norm = jnp.zeros((1, tokens), jnp.float32)
        for m in range(modules):
            turned = wide[pl.ds(m, tokens, stride=modules), :].T
            act, grad = turned[:rank], turned[rank:]
            norm += jnp.sum(act * act, axis=0, keepdims=True) * jnp.sum(
                grad * grad, axis=0, keepdims=True
            )
            p_ref[0, m] = act.astype(jnp.bfloat16)
            p_ref[1, m] = grad.astype(jnp.bfloat16)
        n_ref[...] = jnp.broadcast_to(norm, n_ref.shape)

    if core is None:
        run()
    else:
        pl.when((lax.axis_index("proj") == 0) == (core == 0))(run)


def lane_squares(chunks):
    total = jnp.zeros((GROUP, LANES), jnp.float32)
    for chunk in chunks:
        for k in range(chunk.shape[0]):
            v = chunk[k].astype(jnp.float32)
            total += v * v
    return total


def last_kernel(part, parts, modules, rank, chunk, p_ref, *refs):
    before, o_ref = refs[:-1], refs[-1]
    tokens = p_ref.shape[3]
    own = rank // 2 // parts
    step = min(8, own)
    squares = lane_squares([chunk])
    o_ref[:, tokens:] = before[0][:, tokens:] + squares if before else squares
    for lanes in tiles(tokens):
        acc = before[0][:, lanes] if before else jnp.zeros((GROUP, lanes.stop - lanes.start), jnp.float32)
        for m in range(modules):
            act = p_ref[0, m, 2 * part * own : 2 * (part + 1) * own, lanes].astype(jnp.float32)
            grad = p_ref[1, m, :, lanes]
            for odd in range(2):
                for i in range(0, own, step):
                    k = m * own + i
                    left = chunk[k : k + step].reshape(step * GROUP, LANES)
                    left = left[:, odd * rank : (odd + 1) * rank]
                    inner = jnp.dot(left, grad, preferred_element_type=jnp.float32)
                    for s in range(step):
                        row = 2 * (i + s) + odd
                        acc += inner[s * GROUP : (s + 1) * GROUP] * act[row : row + 1]
        o_ref[:, lanes] = acc


def core_kernel(core, kept, part, parts, modules, rank, chunk, p_ref, *refs):
    def run():
        last_kernel(part, parts, modules, rank, chunk, p_ref, *(refs[1:] if kept else refs))

    if core is None:
        run()
    else:
        pl.when((lax.axis_index("proj") == 0) == (core == 0))(run)


def products(blocks, part, parts, modules, rank, p_ref, lanes):
    own = rank // 2 // parts
    step = min(4, own)
    used = len(blocks) * GROUP
    blocks = (list(blocks) * 8)[: -(-len(blocks) // 8) * 8]
    acc = jnp.zeros((len(blocks) * GROUP, lanes.stop - lanes.start), jnp.float32)
    for m in range(modules):
        grad = p_ref[1, m, :, lanes]
        for i in range(0, own, step):
            k = m * own + i
            row = 2 * (part * own + i)
            left = jnp.concatenate(
                [jnp.concatenate([block[k + s] for block in blocks], axis=0) for s in range(step)],
                axis=1,
            )
            right = jnp.concatenate(
                [grad * p_ref[0, m, row + s : row + s + 1, lanes] for s in range(2 * step)], axis=0
            )
            acc += jnp.dot(left, right, preferred_element_type=jnp.float32)
    return acc[:used]


def tiles(tokens):
    size = 512 if tokens % 512 == 0 else tokens
    return [slice(t, t + size) for t in range(0, tokens, size)]


def early_kernel(count, parts, modules, rank, *refs):
    blocks = refs[:count]
    p_ref, o_ref = refs[count:]
    tokens = p_ref.shape[3]
    for b in range(count):
        o_ref[b * GROUP : (b + 1) * GROUP, tokens:] = lane_squares(blocks[b : b + 1])
    for lanes in tiles(tokens):
        o_ref[:, lanes] = products(blocks, 0, parts, modules, rank, p_ref, lanes)


def late_kernel(count, parts, modules, rank, *refs):
    blocks = refs[:count]
    p_ref, sum_ref, o_ref = refs[count:]
    tokens = p_ref.shape[3]
    known = sum_ref.shape[0]
    for b in range(count):
        o_ref[b * GROUP : (b + 1) * GROUP, tokens:] = lane_squares(blocks[b : b + 1])
    for lanes in tiles(tokens):
        o_ref[:, lanes] = products(blocks, parts - 1, parts, modules, rank, p_ref, lanes)
    o_ref[:known] += sum_ref[...]


def third_kernel(count, parts, modules, rank, ring, chunk, p_ref, n_ref, sum_ref, keep_ref, send_ref, last):
    tokens = p_ref.shape[3]
    half = keep_ref.shape[0] // GROUP
    first = (count - 1) * GROUP
    last_kernel(0, parts, modules, rank, chunk, p_ref, sum_ref.at[first:], last)
    send_ref[half * GROUP :, :tokens] = n_ref[...]
    me = lax.axis_index("proj")
    for b, index in enumerate(ring()):
        rows = last[...] if b == count - 1 else sum_ref[b * GROUP : (b + 1) * GROUP]
        at = pl.multiple_of(lax.rem(index, half) * GROUP, GROUP)

        @pl.when(index // half == me)
        def _():
            keep_ref[pl.ds(at, GROUP), :] = rows

        @pl.when(index // half != me)
        def _():
            send_ref[pl.ds(at, GROUP), :] = rows


def scaled(rows, tokens, width, token_scale):
    square = jnp.sum(rows[:, tokens:], axis=1, keepdims=True)
    return rows[:, :tokens] * lax.rsqrt(square / width + epsilon) * token_scale


def most_kernel(width, keep_ref, far_ref, n_ref, o_ref, s_ref):
    rows, tokens = o_ref.shape
    norm = n_ref[...] + far_ref[rows:, :tokens]
    scale = lax.rsqrt(norm / width + epsilon) / jnp.sqrt(jnp.float32(width))
    s_ref[...] = scale
    o_ref[...] = scaled(keep_ref[...] + far_ref[:rows], tokens, width, scale[:1])


def rest_kernel(width, ring, own_ref, far_ref, s_ref, most_ref, o_ref, rows, sem):
    del most_ref
    tokens = o_ref.shape[1]
    half = o_ref.shape[0] // GROUP
    index = ring()

    @pl.when(index // half == lax.axis_index("proj"))
    def _():
        rows[...] = scaled(own_ref[...] + far_ref[...], tokens, width, s_ref[:1])
        at = pl.multiple_of(lax.rem(index, half) * GROUP, GROUP)
        copy = pltpu.make_async_copy(rows, o_ref.at[pl.ds(at, GROUP), :], sem)
        copy.start()
        copy.wait()


def local(train_factors, query_grads):
    tokens, modules, doubled = train_factors.shape
    rank = doubled // 2
    pairs = rank // 2
    ex, proj = lax.axis_size("ex"), lax.axis_size("proj")
    queries = query_grads.shape[0]
    width = modules * proj * rank * rank
    wide = tokens + LANES
    columns = queries * ex // proj

    token_rows = train_factors.reshape(tokens * modules, doubled)
    def token_work(core, *before):
        return pl.pallas_call(
            functools.partial(token_kernel, modules, rank, core),
            out_shape=(
                jax.ShapeDtypeStruct((2, modules, rank, tokens), jnp.bfloat16),
                jax.ShapeDtypeStruct((8, tokens), jnp.float32),
            ),
            in_specs=[HBM] + [VMEM] * len(before),
            out_specs=(VMEM, VMEM),
            scratch_shapes=[
                pltpu.VMEM((tokens * modules, doubled), jnp.bfloat16),
                pltpu.VMEM((tokens * modules, doubled), jnp.float32),
                pltpu.SemaphoreType.DMA,
            ],
            input_output_aliases={1 + i: i for i in range(len(before))},
            compiler_params=PARAMS,
            name="tokens",
        )(pltpu.with_memory_space_constraint(token_rows, pltpu.HBM), *before)

    def swapped(x):
        return lax.ppermute(x, "proj", [(i, (i + 1) % proj) for i in range(proj)])

    def bulk(blocks, ring, factors, norm):
        count, parts = len(blocks), len(blocks[0])
        early = pl.pallas_call(
            functools.partial(early_kernel, count - 1, parts, modules, rank),
            out_shape=jax.ShapeDtypeStruct(((count - 1) * GROUP, wide), jnp.float32),
            in_specs=[VMEM] * count,
            out_specs=VMEM,
            compiler_params=PARAMS,
            cost_estimate=cover(0.81),
            name="early",
        )(*[block[0] for block in blocks[:-1]], factors)
        late = pl.pallas_call(
            functools.partial(late_kernel, count, parts, modules, rank),
            out_shape=jax.ShapeDtypeStruct((count * GROUP, wide), jnp.float32),
            in_specs=[VMEM] * (count + 2),
            out_specs=VMEM,
            compiler_params=PARAMS,
            cost_estimate=cover(0.58),
            name="late",
        )(*[block[-1] for block in blocks], factors, early)
        return pl.pallas_call(
            functools.partial(third_kernel, count, parts, modules, rank, ring),
            out_shape=(
                jax.ShapeDtypeStruct((columns, wide), jnp.float32),
                jax.ShapeDtypeStruct((columns + 8, wide), jnp.float32),
            ),
            in_specs=[VMEM] * 4,
            out_specs=(VMEM, VMEM),
            scratch_shapes=[pltpu.VMEM((GROUP, wide), jnp.float32)],
            compiler_params=PARAMS,
            cost_estimate=cover(0.23),
            name="third",
        )(blocks[-1][0], factors, norm, late)

    def most(keep, far, norm):
        return pl.pallas_call(
            functools.partial(most_kernel, width),
            out_shape=(
                jax.ShapeDtypeStruct((columns, tokens), jnp.float32),
                jax.ShapeDtypeStruct((8, tokens), jnp.float32),
            ),
            in_specs=[VMEM] * 3,
            out_specs=(VMEM, VMEM),
            compiler_params=PARAMS,
            cost_estimate=LONG,
            name="most",
        )(keep, far, norm)

    if queries == GROUP and ex % 2 == 0 and ex <= 16:
        order = list(range(0, ex, 2)) + list(range(ex - 1, 0, -2))
        order = order[:1] + order[:0:-1]
        up_pairs = [(order[i], order[(i + 1) % ex]) for i in range(ex)]
        down_pairs = [(b, a) for a, b in up_pairs]

        def up(x):
            return lax.ppermute(x, "ex", up_pairs)

        def down(x):
            return lax.ppermute(x, "ex", down_pairs)

        rows = query_grads.reshape(queries, modules, pairs, LANES)
        rows = rows.transpose(0, 2, 1, 3).reshape(queries, pairs * modules, LANES)
        chunk = jax.ShapeDtypeStruct((modules * pairs // 2, queries, LANES), jnp.bfloat16)
        block = pl.pallas_call(
            functools.partial(query_kernel, modules, pairs),
            out_shape=(chunk, chunk),
            in_specs=[HBM],
            out_specs=(VMEM, VMEM),
            scratch_shapes=[
                pltpu.VMEM((2, queries, pairs * modules // 2, LANES), jnp.float32),
                pltpu.SemaphoreType.DMA((2,)),
            ],
            compiler_params=PARAMS,
            name="queries",
        )(pltpu.with_memory_space_constraint(rows, pltpu.HBM))
        factors, norm = token_work(1)
        later = lax.optimization_barrier((block[1], block[0], factors))
        below, above, factors = (block[0], later[0]), (later[1], block[1]), later[2]
        factors, norm = token_work(0, factors, norm)
        blocks, steps = [block], [0]
        for step in range(1, ex // 2):
            first = (up(below[0]), down(above[0]))
            second = (up(below[1]), down(above[1]))
            if step == 2:
                arrived, factors = lax.optimization_barrier((second[0], factors))
                second = (arrived, second[1])
            below, above = (first[0], second[0]), (first[1], second[1])
            blocks += [below, above]
            steps += [-step, step]
        across = (up(below[0]), down(above[1]))

        def ring():
            here = place_of(lax.axis_index("ex"), ex)
            return [index_at(here + step, ex) for step in steps]

        def opposite():
            return index_at(place_of(lax.axis_index("ex"), ex) + ex // 2, ex)

        keep, send = bulk(blocks, ring, factors, norm)
        def scored(part, core, cost, *before):
            kept = part == 0 and bool(before)
            return pl.pallas_call(
                functools.partial(core_kernel, core, kept, part, 2, modules, rank),
                out_shape=jax.ShapeDtypeStruct((GROUP, wide), jnp.float32),
                in_specs=[VMEM] * (2 + len(before)),
                out_specs=VMEM,
                input_output_aliases={2: 0} if kept else {},
                compiler_params=PARAMS,
                cost_estimate=cost,
                name="last",
            )(across[part], factors, *before)

        mine = scored(0, 1, SHORT)
        send, mine = lax.optimization_barrier((send, mine))
        out, scale = most(keep, swapped(send), norm)
        mine = scored(0, 0, cover(0.46), mine)
        mine = scored(1, None, LONG, mine)
        out = pl.pallas_call(
            functools.partial(rest_kernel, width, opposite),
            out_shape=jax.ShapeDtypeStruct((columns, tokens), jnp.float32),
            in_specs=[VMEM, VMEM, VMEM, ANY],
            out_specs=ANY,
            scratch_shapes=[pltpu.VMEM((GROUP, tokens), jnp.float32), pltpu.SemaphoreType.DMA],
            input_output_aliases={3: 0},
            compiler_params=PARAMS,
            name="rest",
        )(mine, swapped(mine), scale, out)
    else:
        gathered = lax.all_gather(query_grads.astype(jnp.bfloat16), "ex", axis=0, tiled=True)
        count = queries * ex // GROUP
        gathered = gathered.reshape(count, GROUP, modules, 2, pairs // 2, LANES)
        gathered = gathered.transpose(0, 3, 2, 4, 1, 5).reshape(count, 2, -1, GROUP, LANES)
        blocks = [(gathered[i, 0], gathered[i, 1]) for i in range(count)]
        factors, norm = token_work(None)
        keep, send = bulk(blocks, lambda: [jnp.int32(i) for i in range(count)], factors, norm)
        out, _ = most(keep, swapped(send), norm)
    return out.T


def solution(mesh):
    return jax.shard_map(
        local,
        mesh=mesh,
        in_specs=(P(("groups", "ex"), "proj", None), P(("groups", "ex"), "proj", None)),
        out_specs=P(("groups", "ex"), "proj"),
        check_vma=False,
    )
```

```python
import functools

import jax
import jax.numpy as jnp
from jax import lax
from jax.experimental import pallas as pl
from jax.experimental.pallas import tpu as pltpu
from jax.sharding import PartitionSpec as P

epsilon = 1e-06
LANES = 128
GROUP = 16
VMEM = pl.BlockSpec(memory_space=pltpu.VMEM)
HBM = pl.BlockSpec(memory_space=pltpu.HBM)


SHORT = pl.CostEstimate(flops=10**6, bytes_accessed=1024, transcendentals=0)


def cover(share):
    return pl.CostEstimate(flops=int(share * 10**9), bytes_accessed=1024, transcendentals=0)


ANY = pl.BlockSpec(memory_space=pl.ANY)
PARAMS = pltpu.CompilerParams(vmem_limit_bytes=16 * 1024 * 1024)
LONG = pl.CostEstimate(flops=10**10, bytes_accessed=4 * 1024 * 1024, transcendentals=0)


def place_of(index, count):
    return lax.rem(count - jnp.where(index % 2 == 0, index // 2, count - (index + 1) // 2), count)


def index_at(place, count):
    place = lax.rem(2 * count - place, count)
    return jnp.where(place < count // 2, 2 * place, 2 * (count - place) - 1)


def query_kernel(modules, pairs, x_ref, *refs):
    chunks, rows, sems = refs[:-2], refs[-2], refs[-1]
    queries = chunks[0].shape[1]
    own = pairs // len(chunks)
    span = own * modules
    copy = pltpu.make_async_copy(x_ref, rows, sems)
    copy.start()
    copy.wait()
    flat = rows.reshape(queries * span * len(chunks), LANES)
    for c, o_ref in enumerate(chunks):
        for m in range(modules):
            for i in range(own):
                got = flat[pl.ds(c * span + i * modules + m, queries, stride=span * len(chunks)), :]
                o_ref[m * own + i] = got.astype(jnp.bfloat16)


def token_kernel(modules, rank, core, x_ref, *refs):
    p_ref, n_ref, rows, wide, sem = refs[-5:]
    tokens = x_ref.shape[0] // modules

    def run():
        copy = pltpu.make_async_copy(x_ref, rows, sem)
        copy.start()
        copy.wait()
        wide[...] = rows[...].astype(jnp.float32)
        norm = jnp.zeros((1, tokens), jnp.float32)
        for m in range(modules):
            turned = wide[pl.ds(m, tokens, stride=modules), :].T
            act, grad = turned[:rank], turned[rank:]
            norm += jnp.sum(act * act, axis=0, keepdims=True) * jnp.sum(
                grad * grad, axis=0, keepdims=True
            )
            p_ref[0, m] = act.astype(jnp.bfloat16)
            p_ref[1, m] = grad.astype(jnp.bfloat16)
        n_ref[...] = jnp.broadcast_to(norm, n_ref.shape)

    if core is None:
        run()
    else:
        pl.when((lax.axis_index("proj") == 0) == (core == 0))(run)


def lane_squares(chunks):
    total = jnp.zeros((GROUP, LANES), jnp.float32)
    for chunk in chunks:
        for k in range(chunk.shape[0]):
            v = chunk[k].astype(jnp.float32)
            total += v * v
    return total


def last_kernel(part, parts, modules, rank, chunk, p_ref, *refs):
    before, o_ref = refs[:-1], refs[-1]
    tokens = p_ref.shape[3]
    own = rank // 2 // parts
    step = min(8, own)
    squares = lane_squares([chunk])
    o_ref[:, tokens:] = before[0][:, tokens:] + squares if before else squares
    for lanes in tiles(tokens):
        acc = before[0][:, lanes] if before else jnp.zeros((GROUP, lanes.stop - lanes.start), jnp.float32)
        for m in range(modules):
            act = p_ref[0, m, 2 * part * own : 2 * (part + 1) * own, lanes].astype(jnp.float32)
            grad = p_ref[1, m, :, lanes]
            for odd in range(2):
                for i in range(0, own, step):
                    k = m * own + i
                    left = chunk[k : k + step].reshape(step * GROUP, LANES)
                    left = left[:, odd * rank : (odd + 1) * rank]
                    inner = jnp.dot(left, grad, preferred_element_type=jnp.float32)
                    for s in range(step):
                        row = 2 * (i + s) + odd
                        acc += inner[s * GROUP : (s + 1) * GROUP] * act[row : row + 1]
        o_ref[:, lanes] = acc


def core_kernel(core, kept, part, parts, modules, rank, chunk, p_ref, *refs):
    def run():
        last_kernel(part, parts, modules, rank, chunk, p_ref, *(refs[1:] if kept else refs))

    if core is None:
        run()
    else:
        pl.when((lax.axis_index("proj") == 0) == (core == 0))(run)


def products(blocks, part, parts, modules, rank, p_ref, lanes):
    own = rank // 2 // parts
    step = min(4, own)
    used = len(blocks) * GROUP
    blocks = (list(blocks) * 8)[: -(-len(blocks) // 8) * 8]
    acc = jnp.zeros((len(blocks) * GROUP, lanes.stop - lanes.start), jnp.float32)
    for m in range(modules):
        grad = p_ref[1, m, :, lanes]
        for i in range(0, own, step):
            k = m * own + i
            row = 2 * (part * own + i)
            left = jnp.concatenate(
                [jnp.concatenate([block[k + s] for block in blocks], axis=0) for s in range(step)],
                axis=1,
            )
            right = jnp.concatenate(
                [grad * p_ref[0, m, row + s : row + s + 1, lanes] for s in range(2 * step)], axis=0
            )
            acc += jnp.dot(left, right, preferred_element_type=jnp.float32)
    return acc[:used]


def tiles(tokens):
    size = 512 if tokens % 512 == 0 else tokens
    return [slice(t, t + size) for t in range(0, tokens, size)]


def early_kernel(count, parts, modules, rank, *refs):
    blocks = refs[:count]
    p_ref, o_ref = refs[count:]
    tokens = p_ref.shape[3]
    for b in range(count):
        o_ref[b * GROUP : (b + 1) * GROUP, tokens:] = lane_squares(blocks[b : b + 1])
    for lanes in tiles(tokens):
        o_ref[:, lanes] = products(blocks, 0, parts, modules, rank, p_ref, lanes)


def late_kernel(count, parts, modules, rank, *refs):
    blocks = refs[:count]
    p_ref, sum_ref, o_ref = refs[count:]
    tokens = p_ref.shape[3]
    known = sum_ref.shape[0]
    for b in range(count):
        o_ref[b * GROUP : (b + 1) * GROUP, tokens:] = lane_squares(blocks[b : b + 1])
    for lanes in tiles(tokens):
        o_ref[:, lanes] = products(blocks, parts - 1, parts, modules, rank, p_ref, lanes)
    o_ref[:known] += sum_ref[...]


def third_kernel(count, parts, modules, rank, ring, chunk, p_ref, n_ref, sum_ref, keep_ref, send_ref, last):
    tokens = p_ref.shape[3]
    half = keep_ref.shape[0] // GROUP
    first = (count - 1) * GROUP
    last_kernel(0, parts, modules, rank, chunk, p_ref, sum_ref.at[first:], last)
    send_ref[half * GROUP :, :tokens] = n_ref[...]
    me = lax.axis_index("proj")
    for b, index in enumerate(ring()):
        rows = last[...] if b == count - 1 else sum_ref[b * GROUP : (b + 1) * GROUP]
        at = pl.multiple_of(lax.rem(index, half) * GROUP, GROUP)

        @pl.when(index // half == me)
        def _():
            keep_ref[pl.ds(at, GROUP), :] = rows

        @pl.when(index // half != me)
        def _():
            send_ref[pl.ds(at, GROUP), :] = rows


def scaled(rows, tokens, width, token_scale):
    square = jnp.sum(rows[:, tokens:], axis=1, keepdims=True)
    return rows[:, :tokens] * lax.rsqrt(square / width + epsilon) * token_scale


def most_kernel(width, keep_ref, far_ref, n_ref, o_ref, s_ref):
    rows, tokens = o_ref.shape
    norm = n_ref[...] + far_ref[rows:, :tokens]
    scale = lax.rsqrt(norm / width + epsilon) / jnp.sqrt(jnp.float32(width))
    s_ref[...] = scale
    o_ref[...] = scaled(keep_ref[...] + far_ref[:rows], tokens, width, scale[:1])


def rest_kernel(width, ring, own_ref, far_ref, s_ref, most_ref, o_ref, rows, sem):
    del most_ref
    tokens = o_ref.shape[1]
    half = o_ref.shape[0] // GROUP
    index = ring()

    @pl.when(index // half == lax.axis_index("proj"))
    def _():
        rows[...] = scaled(own_ref[...] + far_ref[...], tokens, width, s_ref[:1])
        at = pl.multiple_of(lax.rem(index, half) * GROUP, GROUP)
        copy = pltpu.make_async_copy(rows, o_ref.at[pl.ds(at, GROUP), :], sem)
        copy.start()
        copy.wait()


def local(train_factors, query_grads):
    tokens, modules, doubled = train_factors.shape
    rank = doubled // 2
    pairs = rank // 2
    ex, proj = lax.axis_size("ex"), lax.axis_size("proj")
    queries = query_grads.shape[0]
    width = modules * proj * rank * rank
    wide = tokens + LANES
    columns = queries * ex // proj

    token_rows = train_factors.reshape(tokens * modules, doubled)
    def token_work(core, *before):
        return pl.pallas_call(
            functools.partial(token_kernel, modules, rank, core),
            out_shape=(
                jax.ShapeDtypeStruct((2, modules, rank, tokens), jnp.bfloat16),
                jax.ShapeDtypeStruct((8, tokens), jnp.float32),
            ),
            in_specs=[HBM] + [VMEM] * len(before),
            out_specs=(VMEM, VMEM),
            scratch_shapes=[
                pltpu.VMEM((tokens * modules, doubled), jnp.bfloat16),
                pltpu.VMEM((tokens * modules, doubled), jnp.float32),
                pltpu.SemaphoreType.DMA,
            ],
            input_output_aliases={1 + i: i for i in range(len(before))},
            compiler_params=PARAMS,
            name="tokens",
        )(pltpu.with_memory_space_constraint(token_rows, pltpu.HBM), *before)

    def swapped(x):
        return lax.ppermute(x, "proj", [(i, (i + 1) % proj) for i in range(proj)])

    def bulk(blocks, ring, factors, norm):
        count, parts = len(blocks), len(blocks[0])
        early = pl.pallas_call(
            functools.partial(early_kernel, count - 1, parts, modules, rank),
            out_shape=jax.ShapeDtypeStruct(((count - 1) * GROUP, wide), jnp.float32),
            in_specs=[VMEM] * count,
            out_specs=VMEM,
            compiler_params=PARAMS,
            cost_estimate=cover(0.81),
            name="early",
        )(*[block[0] for block in blocks[:-1]], factors)
        late = pl.pallas_call(
            functools.partial(late_kernel, count, parts, modules, rank),
            out_shape=jax.ShapeDtypeStruct((count * GROUP, wide), jnp.float32),
            in_specs=[VMEM] * (count + 2),
            out_specs=VMEM,
            compiler_params=PARAMS,
            cost_estimate=cover(0.58),
            name="late",
        )(*[block[-1] for block in blocks], factors, early)
        return pl.pallas_call(
            functools.partial(third_kernel, count, parts, modules, rank, ring),
            out_shape=(
                jax.ShapeDtypeStruct((columns, wide), jnp.float32),
                jax.ShapeDtypeStruct((columns + 8, wide), jnp.float32),
            ),
            in_specs=[VMEM] * 4,
            out_specs=(VMEM, VMEM),
            scratch_shapes=[pltpu.VMEM((GROUP, wide), jnp.float32)],
            compiler_params=PARAMS,
            cost_estimate=cover(0.23),
            name="third",
        )(blocks[-1][0], factors, norm, late)

    def most(keep, far, norm):
        return pl.pallas_call(
            functools.partial(most_kernel, width),
            out_shape=(
                jax.ShapeDtypeStruct((columns, tokens), jnp.float32),
                jax.ShapeDtypeStruct((8, tokens), jnp.float32),
            ),
            in_specs=[VMEM] * 3,
            out_specs=(VMEM, VMEM),
            compiler_params=PARAMS,
            cost_estimate=LONG,
            name="most",
        )(keep, far, norm)

    if queries == GROUP and ex % 2 == 0 and ex <= 16:
        order = list(range(0, ex, 2)) + list(range(ex - 1, 0, -2))
        order = order[:1] + order[:0:-1]
        up_pairs = [(order[i], order[(i + 1) % ex]) for i in range(ex)]
        down_pairs = [(b, a) for a, b in up_pairs]

        def up(x):
            return lax.ppermute(x, "ex", up_pairs)

        def down(x):
            return lax.ppermute(x, "ex", down_pairs)

        rows = query_grads.reshape(queries, modules, pairs, LANES)
        rows = rows.transpose(0, 2, 1, 3).reshape(queries, pairs * modules, LANES)
        chunk = jax.ShapeDtypeStruct((modules * pairs // 2, queries, LANES), jnp.bfloat16)
        block = pl.pallas_call(
            functools.partial(query_kernel, modules, pairs),
            out_shape=(chunk, chunk),
            in_specs=[HBM],
            out_specs=(VMEM, VMEM),
            scratch_shapes=[
                pltpu.VMEM((queries, pairs * modules, LANES), jnp.float32),
                pltpu.SemaphoreType.DMA,
            ],
            compiler_params=PARAMS,
            name="queries",
        )(pltpu.with_memory_space_constraint(rows, pltpu.HBM))
        factors, norm = token_work(1)
        later = lax.optimization_barrier((block[1], block[0], factors))
        below, above, factors = (block[0], later[0]), (later[1], block[1]), later[2]
        factors, norm = token_work(0, factors, norm)
        blocks, steps = [block], [0]
        for step in range(1, ex // 2):
            first = (up(below[0]), down(above[0]))
            second = (up(below[1]), down(above[1]))
            if step == 2:
                arrived, factors = lax.optimization_barrier((second[0], factors))
                second = (arrived, second[1])
            below, above = (first[0], second[0]), (first[1], second[1])
            blocks += [below, above]
            steps += [-step, step]
        across = (up(below[0]), down(above[1]))

        def ring():
            here = place_of(lax.axis_index("ex"), ex)
            return [index_at(here + step, ex) for step in steps]

        def opposite():
            return index_at(place_of(lax.axis_index("ex"), ex) + ex // 2, ex)

        keep, send = bulk(blocks, ring, factors, norm)
        def scored(part, core, cost, *before):
            kept = part == 0 and bool(before)
            return pl.pallas_call(
                functools.partial(core_kernel, core, kept, part, 2, modules, rank),
                out_shape=jax.ShapeDtypeStruct((GROUP, wide), jnp.float32),
                in_specs=[VMEM] * (2 + len(before)),
                out_specs=VMEM,
                input_output_aliases={2: 0} if kept else {},
                compiler_params=PARAMS,
                cost_estimate=cost,
                name="last",
            )(across[part], factors, *before)

        mine = scored(0, 1, SHORT)
        send, mine = lax.optimization_barrier((send, mine))
        out, scale = most(keep, swapped(send), norm)
        mine = scored(0, 0, cover(0.46), mine)
        mine = scored(1, None, LONG, mine)
        out = pl.pallas_call(
            functools.partial(rest_kernel, width, opposite),
            out_shape=jax.ShapeDtypeStruct((columns, tokens), jnp.float32),
            in_specs=[VMEM, VMEM, VMEM, ANY],
            out_specs=ANY,
            scratch_shapes=[pltpu.VMEM((GROUP, tokens), jnp.float32), pltpu.SemaphoreType.DMA],
            input_output_aliases={3: 0},
            compiler_params=PARAMS,
            name="rest",
        )(mine, swapped(mine), scale, out)
    else:
        gathered = lax.all_gather(query_grads.astype(jnp.bfloat16), "ex", axis=0, tiled=True)
        count = queries * ex // GROUP
        gathered = gathered.reshape(count, GROUP, modules, 2, pairs // 2, LANES)
        gathered = gathered.transpose(0, 3, 2, 4, 1, 5).reshape(count, 2, -1, GROUP, LANES)
        blocks = [(gathered[i, 0], gathered[i, 1]) for i in range(count)]
        factors, norm = token_work(None)
        keep, send = bulk(blocks, lambda: [jnp.int32(i) for i in range(count)], factors, norm)
        out, _ = most(keep, swapped(send), norm)
    return out.T


def solution(mesh):
    return jax.shard_map(
        local,
        mesh=mesh,
        in_specs=(P(("groups", "ex"), "proj", None), P(("groups", "ex"), "proj", None)),
        out_specs=P(("groups", "ex"), "proj"),
        check_vma=False,
    )
```
